256 devices in a mesh: grp: 8 (over z_lo, core), exp: 32 (over z_hi, y, x).
Axes of the slice: x: 4, y: 4, z: 8 (z_hi: 2, z_lo: 4; z = z_hi * 4 + z_lo), core: 2. Of those that a mesh axis runs over, the one named last changes fastest.
Arguments:
- tokens: bfloat16 [8192, 7168], P('exp', 'grp'), may hold values from -6 to 6
- d_out: bfloat16 [8192, 7168], P('exp', 'grp'), may hold values from -6 to 6
- row_expert: int32 [8192], P('exp'), may hold values from 0 to 31, as said below
- w_gate_up: bfloat16 [32, 7168, 2, 1024], P('exp', 'grp'), may hold values from -0.0625 to 0.0625
- w_down: bfloat16 [32, 1024, 7168], P('exp', None, 'grp'), may hold values from -0.1875 to 0.1875
Outputs:
- token_grads: bfloat16 [8192, 7168], P('exp', 'grp')
- gate_up_grads: bfloat16 [32, 7168, 2, 1024], P('exp', 'grp')
- down_grads: bfloat16 [32, 1024, 7168], P('exp', None, 'grp')
The draws below stay inside these ranges and needn't reach their ends.
Inputs may be any that keep to these rules, and one draw needn't show every extreme that they name: `row_expert`: in each block of 256 rows held by one index of exp, one expert, the same for every block, is named by exactly 32 rows; every other expert by at most 16 rows, and in every block some expert by exactly 16.
All inputs are finite; a program needn't handle non-finite values.
Results may differ from the reference program's by a relative error of at most 0.028.
Values may be sent and summed in bfloat16 or wider, within the bound.
A program may use at most 128 MiB of HBM per device.

```python
import jax
import jax.numpy as jnp
from jax import lax

D = 7168
HIDDEN_SIZE = 1024
ROWS_DEV = 256
EXPERTS = 32
TOKENS = 8192
CAP = 16
HOT_CAP = 32
N_GRP = 8
N_EXP = 32


def draw_row_expert(key, part):
    key = jax.random.fold_in(key, 11)
    hot_key, block_key = jax.random.split(key)
    hot_expert = jax.random.randint(hot_key, (), 0, N_EXP)
    cold_cap = 2 * ROWS_DEV // N_EXP
    hot_cap = 4 * ROWS_DEV // N_EXP
    cold_rows = ROWS_DEV - hot_cap
    slot_total = (N_EXP - 1) * cold_cap

    def one_block(block_number):
        one_key = jax.random.fold_in(block_key, block_number)
        first_key, second_key, third_key = jax.random.split(one_key, 3)
        full_cold = jax.random.randint(first_key, (), 0, N_EXP - 1)
        slot_owner = jnp.arange(slot_total, dtype=jnp.int32) // cold_cap
        random_part = jax.random.randint(second_key, (slot_total,), 0, 1 << 16)
        positions = jnp.arange(slot_total, dtype=jnp.int32)
        sort_score = random_part * slot_total + positions
        sort_score = jnp.where(slot_owner == full_cold, positions - slot_total, sort_score)
        slot_order = jnp.argsort(sort_score)
        chosen = slot_owner[slot_order[:cold_rows]]
        chosen = jnp.where(chosen >= hot_expert, chosen + 1, chosen)
        source_rows = jnp.concatenate([jnp.full((hot_cap,), hot_expert, dtype=jnp.int32), chosen.astype(jnp.int32)])
        return jax.random.permutation(third_key, source_rows)
    return jax.vmap(one_block)(jnp.arange(N_EXP)).reshape(-1).astype(jnp.int32)


def block_scale(key, extent, cuts, smallest, high):
    def one(position, parts):
        heights = jax.random.uniform(jax.random.fold_in(jax.random.fold_in(key, 6), position), (parts,), jnp.float32, smallest / len(cuts), high / len(cuts))
        return jnp.repeat(jnp.exp(heights), extent[position] // parts).reshape((-1,) + (1,) * (len(extent) - position - 1))

    level = one(*cuts[0])
    for cut in cuts[1:]:
        level = level * one(*cut)
    return level


def centred(stream_key, extent, scale, limit, cuts=(), kind=jnp.bfloat16):
    values = scale * jax.random.normal(stream_key, extent, jnp.float32)
    if cuts:
        values = values * block_scale(stream_key, extent, cuts, -0.22, 0.18)
    return jnp.clip(values, -limit, limit).astype(kind)


def setup_inputs(seed: int = 0) -> dict:
    splits = jax.random.split(jax.random.key(seed), 6)
    tokens = centred(splits[0], (TOKENS, D), 1.0, 6.0, ((0, 32), (1, 8)))
    d_out = centred(splits[1], (TOKENS, D), 1.0, 6.0, ((0, 32), (1, 8)))
    row_expert = draw_row_expert(jax.random.fold_in(splits[5], 71), 0)
    w_gate_up = centred(splits[3], (EXPERTS, D, 2, HIDDEN_SIZE), D ** -0.5, 0.0625, ((0, 32), (1, 8)))
    w_down = centred(splits[4], (EXPERTS, HIDDEN_SIZE, D), HIDDEN_SIZE ** -0.5, 0.1875, ((0, 32), (2, 8)))
    return dict(tokens=tokens, d_out=d_out, row_expert=row_expert, w_gate_up=w_gate_up, w_down=w_down)


def silu_parts(gate_value):
    sigmoid_value = jax.nn.sigmoid(gate_value)
    return gate_value * sigmoid_value, sigmoid_value * (1.0 + gate_value * (1.0 - sigmoid_value))


def blocked_product(left, right):
    block_rows = left.shape[0]
    feature_share = D // N_GRP
    left_blocks = left.reshape(block_rows, N_GRP, feature_share).astype(jnp.float32)
    right_blocks = right.reshape(N_GRP, feature_share, right.shape[1]).astype(jnp.float32)
    partials = jnp.einsum("bgk,gkn->gbn", left_blocks, right_blocks).astype(jnp.bfloat16)
    partials = lax.optimization_barrier(partials)
    return jnp.sum(partials.astype(jnp.float32), axis=0)


def expert_block(tokens, d_out, w_gate_up, w_down, row_order, start_row, row_total, expert, block_rows):
    row_index = lax.dynamic_slice_in_dim(row_order, start_row.astype(jnp.int32), block_rows)
    is_valid = (jnp.arange(block_rows, dtype=jnp.int32) < row_total)[:, None]
    block_tokens = jnp.where(is_valid, tokens[row_index], jnp.zeros((), tokens.dtype))
    block_grads = jnp.where(is_valid, d_out[row_index], jnp.zeros((), d_out.dtype))
    gate_up_matrix = w_gate_up[expert].reshape(D, 2 * HIDDEN_SIZE)
    down_matrix = w_down[expert]
    gate_up = blocked_product(block_tokens, gate_up_matrix)
    hidden_grads = blocked_product(block_grads, jnp.transpose(down_matrix))
    activated, gate_slope = silu_parts(gate_up[:, :HIDDEN_SIZE])
    upward = gate_up[:, HIDDEN_SIZE:]
    hidden = (activated * upward).astype(jnp.bfloat16)
    branch_grads = jnp.concatenate([hidden_grads * upward * gate_slope, hidden_grads * activated], axis=1).astype(jnp.bfloat16)
    down_grads = lax.dot_general(hidden, block_grads, (((0,), (0,)), ((), ())), preferred_element_type=jnp.float32).astype(jnp.bfloat16)
    gate_up_grads = lax.dot_general(block_tokens, branch_grads, (((0,), (0,)), ((), ())), preferred_element_type=jnp.float32).astype(jnp.bfloat16).reshape(D, 2, HIDDEN_SIZE)
    row_grads = lax.dot_general(branch_grads, gate_up_matrix, (((1,), (1,)), ((), ())), preferred_element_type=jnp.float32).astype(jnp.bfloat16)
    row_grads = jnp.where(is_valid, row_grads, jnp.zeros((), row_grads.dtype))
    return row_index, row_grads, gate_up_grads, down_grads


def reference(tokens, d_out, row_expert, w_gate_up, w_down):
    total = tokens.shape[0]
    expert_ids = jnp.arange(EXPERTS, dtype=jnp.int32)
    expert_loads = jnp.sum((row_expert[:, None] == expert_ids[None, :]).astype(jnp.int32), axis=0).astype(jnp.int32)
    expert_starts = (jnp.cumsum(expert_loads) - expert_loads).astype(jnp.int32)
    sort_keys = row_expert.astype(jnp.int32) * total + jnp.arange(total, dtype=jnp.int32)
    row_order = jnp.argsort(sort_keys).astype(jnp.int32)
    hot_block = N_EXP * HOT_CAP
    cold_block = N_EXP * CAP
    row_order = jnp.concatenate([row_order, jnp.zeros((hot_block,), jnp.int32)])
    hot_expert = jnp.argmax(expert_loads).astype(jnp.int32)

    def cold_step(token_grads, expert):
        row_total = jnp.where(expert == hot_expert, 0, expert_loads[expert]).astype(jnp.int32)
        row_index, row_grads, gate_up_grads, down_grads = expert_block(tokens, d_out, w_gate_up, w_down, row_order, expert_starts[expert], row_total, expert, cold_block)
        return token_grads.at[row_index].add(row_grads), (gate_up_grads, down_grads)

    token_grads, (gate_up_all, down_all) = lax.scan(cold_step, jnp.zeros_like(tokens), expert_ids)
    row_index, row_grads, hot_gate_up, hot_down = expert_block(tokens, d_out, w_gate_up, w_down, row_order, expert_starts[hot_expert], expert_loads[hot_expert], hot_expert, hot_block)
    token_grads = token_grads.at[row_index].add(row_grads)
    gate_up_all = gate_up_all.at[hot_expert].set(hot_gate_up)
    down_all = down_all.at[hot_expert].set(hot_down)
    return token_grads, gate_up_all, down_all
```

```python
import jax
import jax.numpy as jnp
from jax import lax
from jax.experimental import pallas as pl
from jax.experimental.pallas import tpu as pltpu
from jax.sharding import PartitionSpec as P

MESH = pl.DeviceIdType.MESH
F32 = jnp.float32
BF16 = jnp.bfloat16

ROWS = 256
FEAT = 896
HID = 1024
WIDE = 3 * HID
N_EXP = 32
HALF = 16
CAP = 16
BASE = N_EXP * CAP
SLOTS = 2 * BASE
CHUNKS = 4
CHUNK = SLOTS // CHUNKS
SHARE = CHUNK // 2
UNIT = SHARE // 4
TILE = 512

NN = (((1,), (0,)), ((), ()))
NT = (((1,), (1,)), ((), ()))
TN = (((0,), (0,)), ((), ()))


def mm(a, b, dims=NN):
    return lax.dot_general(a, b, dims, preferred_element_type=F32)


def rows(start, size):
    return pl.ds(pl.multiple_of(start, 16), size)


def kernel(
    expert_ref, tok_ref, dout_ref, wgu_hbm, wd_hbm,
    tg_ref, gug_ref, dg_ref,
    wgu, wd, xin, din, sendx, sendd, ovx, ovd, csend, crecv, acc,
    rs_send, rs_recv, hb, rowg, back, backo, zsend, zrecv, slots, hotm,
    w_sem, base_send, base_recv, ovz_send, ovz_recv, ov_send, ov_recv, c_send, c_recv,
    rs_s, rs_r, ag_s, ag_r, ret_s, ret_r, reto_s, reto_r, retz_s, retz_r,
):
    me_e = lax.axis_index("exp")
    me_g = lax.axis_index("grp")
    z = me_g // 2
    core = lax.rem(me_g, 2)
    half = me_e // HALF
    q = lax.rem(me_e, HALF)
    z_partner = {"exp": lax.rem(me_e + HALF, N_EXP)}
    core_partner = {"grp": me_g + 1 - 2 * core}
    right = {"grp": lax.rem(me_g + 2, 8)}
    left = {"grp": lax.rem(me_g + 6, 8)}

    def remote(src, dst, s_sem, r_sem, dev):
        return pltpu.make_async_remote_copy(
            src_ref=src, dst_ref=dst, send_sem=s_sem, recv_sem=r_sem, device_id=dev, device_id_type=MESH
        )

    def place(s):
        return (lax.rem(s, HALF) // 8) * 16 + (s // HALF) * 8 + lax.rem(s, 8)

    w1 = pltpu.make_async_copy(wgu_hbm, wgu, w_sem.at[0])
    w2 = pltpu.make_async_copy(wd_hbm, wd, w_sem.at[1])
    w1.start()
    w2.start()
    barrier = pltpu.get_barrier_semaphore()

    @pl.loop(1, N_EXP)
    def _(p):
        pl.semaphore_signal(
            barrier, inc=1, device_id={"exp": lax.rem(me_e + p, N_EXP)}, device_id_type=MESH
        )

    @pl.loop(1, 8)
    def _(p):
        pl.semaphore_signal(barrier, inc=1, device_id={"grp": lax.rem(me_g + p, 8)}, device_id_type=MESH)

    expert = expert_ref[...]
    e_iota = lax.broadcasted_iota(jnp.int32, (N_EXP, ROWS), 0)
    mine = (expert == e_iota).astype(F32)
    upto = (
        lax.broadcasted_iota(jnp.int32, (ROWS, ROWS), 0) <= lax.broadcasted_iota(jnp.int32, (ROWS, ROWS), 1)
    ).astype(F32).astype(BF16)
    running = mm(mine.astype(BF16), upto)
    rank = jnp.sum(running * mine, axis=0, keepdims=True) - 1.0
    slot = jnp.where(rank < CAP, expert.astype(F32) * CAP + rank, -1.0)
    over = rank - CAP
    slots[0:1, :] = slot
    slots[1:2, :] = over
    loads = jnp.sum(mine, axis=1, keepdims=True)
    is_me = (lax.broadcasted_iota(jnp.int32, (N_EXP, 1), 0) == me_e).astype(F32)
    hot = jnp.sum(jnp.where(loads > CAP + 0.5, 1.0, 0.0) * is_me, axis=0, keepdims=True)
    hotm[...] = jnp.broadcast_to(hot, (16, FEAT)).astype(BF16)

    def picks(start, size, values):
        at = lax.broadcasted_iota(jnp.int32, (size, ROWS), 0).astype(F32) + start
        return (at == values).astype(F32).astype(BF16)

    over_pick = picks(0.0, CAP, over)
    ovx[0:CAP, :] = mm(over_pick, tok_ref[...]).astype(BF16)
    ovd[0:CAP, :] = mm(over_pick, dout_ref[...]).astype(BF16)
    for b in range(BASE // 128):
        pick = picks(128.0 * b, 128, slot)
        sendx[b * 128 : (b + 1) * 128, :] = mm(pick, tok_ref[...]).astype(BF16)
        sendd[b * 128 : (b + 1) * 128, :] = mm(pick, dout_ref[...]).astype(BF16)
    pl.semaphore_wait(barrier, N_EXP - 1 + 7)

    ovz = [
        remote(buf.at[pl.ds(0, CAP)], buf.at[pl.ds(CAP, CAP)], ovz_send.at[n], ovz_recv.at[n], z_partner)
        for n, buf in enumerate((ovx, ovd))
    ]
    for copy in ovz:
        copy.start()
    my_place = place(me_e) * CAP

    @pl.loop(1, N_EXP)
    def _(p):
        to = lax.rem(me_e + p, N_EXP)
        for n, (src, dst) in enumerate(((sendx, xin), (sendd, din))):
            remote(
                src.at[rows(to * CAP, CAP)], dst.at[rows(my_place, CAP)],
                base_send.at[n], base_recv.at[n], {"exp": to},
            ).start()

    xin[rows(my_place, CAP), :] = sendx[rows(me_e * CAP, CAP), :]
    din[rows(my_place, CAP), :] = sendd[rows(me_e * CAP, CAP), :]
    for copy in ovz:
        copy.wait_recv()
    over_place = BASE + q * 2 * CAP

    @pl.loop(1, HALF)
    def _(p):
        to = half * HALF + lax.rem(q + p, HALF)
        for n, (src, dst) in enumerate(((ovx, xin), (ovd, din))):
            remote(
                src, dst.at[rows(over_place, 2 * CAP)], ov_send.at[n], ov_recv.at[n], {"exp": to}
            ).start()

    xin[rows(over_place, 2 * CAP), :] = ovx[...]
    din[rows(over_place, 2 * CAP), :] = ovd[...]

    def many(buf, count, s_sem, r_sem):
        part = buf.at[pl.ds(0, count)]
        return remote(part, part, s_sem, r_sem, z_partner)

    w1.wait()
    w2.wait()
    many(xin, BASE - CAP, base_send.at[0], base_recv.at[0]).wait_recv()
    many(din, BASE - CAP, base_send.at[1], base_recv.at[1]).wait_recv()

    ends = []

    def partials(k, mine_too):
        start = k * CHUNK + SHARE * (core if mine_too else 1 - core)

        def put(value, col):
            if mine_too:
                acc[pl.ds(k * SHARE, SHARE), col] = value
            else:
                csend[pl.ds(k * SHARE, SHARE), col] = value.astype(BF16)

        @pl.loop(0, 2 * HID // TILE)
        def _(n):
            col = pl.ds(pl.multiple_of(n * TILE, TILE), TILE)
            put(mm(xin[rows(start, SHARE), :], wgu[:, col]), col)

        @pl.loop(0, HID // TILE)
        def _(n):
            out = pl.ds(pl.multiple_of(2 * HID + n * TILE, TILE), TILE)
            put(mm(din[rows(start, SHARE), :], wd[rows(n * TILE, TILE), :], NT), out)

    def core_copy(k):
        part = pl.ds(k * SHARE, SHARE)
        return remote(csend.at[part], crecv.at[part], c_send.at[k], c_recv.at[k], core_partner)

    def stage_p(k):
        partials(k, False)
        core_copy(k).start()
        partials(k, True)

    def stage_c(k):
        core_copy(k).wait_recv()

        @pl.loop(0, SHARE // 16)
        def _(n):
            at = rows(k * SHARE + n * 16, 16)
            acc[at, :] += crecv[at, :].astype(F32)

    def rs_copy(k, way, d):
        part = pl.ds(((k * 2 + way) * 4 + d) * UNIT, UNIT)
        return remote(
            rs_send.at[part], rs_recv.at[part], rs_s.at[k, way, d], rs_r.at[k, way, d], (right, left)[way]
        )


    def rs_forward(k, way, d, first):
        at = k * SHARE + d * UNIT
        part = ((k * 2 + way) * 4 + d) * UNIT
        copy = rs_copy(k, way, d)
        if not first:
            copy.wait_recv()

        @pl.loop(0, UNIT // 16)
        def _(n):
            value = acc[rows(at + n * 16, 16), :]
            if not first:
                value = value + rs_recv[rows(part + n * 16, 16), :].astype(F32)
            rs_send[rows(part + n * 16, 16), :] = value.astype(BF16)

        copy.start()

    def stage_e(k):
        @pl.when(z == 0)
        def _():
            for d in (3, 2, 1):
                rs_forward(k, 0, d, True)

        @pl.when(z == 3)
        def _():
            for d in (0, 1, 2):
                rs_forward(k, 1, d, True)

    def stage_m(k):
        @pl.when(z == 1)
        def _():
            rs_forward(k, 0, 3, False)
            rs_forward(k, 0, 2, False)
            rs_forward(k, 1, 0, False)

        @pl.when(z == 2)
        def _():
            rs_forward(k, 1, 0, False)
            rs_forward(k, 1, 1, False)
            rs_forward(k, 0, 3, False)

    def ag_copy(k, way, j):
        part = rows(k * CHUNK + core * SHARE + j * UNIT, UNIT)
        return remote(
            hb.at[part], hb.at[part], ag_s.at[k, way, j], ag_r.at[k, core, j], (right, left, core_partner)[way]
        )

    def stage_f(k):
        at = k * SHARE + z * UNIT

        def fold(way):
            dyn = rows(((k * 2 + way) * 4 + z) * UNIT, UNIT)
            remote(
                rs_send.at[dyn], rs_recv.at[dyn], rs_s.at[k, way, z], rs_r.at[k, way, z], (right, left)[way]
            ).wait_recv()
            acc[rows(at, UNIT), :] += rs_recv[dyn, :].astype(F32)

        @pl.when(z > 0)
        def _():
            fold(0)

        @pl.when(z < 3)
        def _():
            fold(1)

        out = rows(k * CHUNK + core * SHARE + z * UNIT, UNIT)

        @pl.loop(0, HID // 256)
        def _(n):
            c0 = pl.multiple_of(n * 256, 256)
            gate = acc[rows(at, UNIT), pl.ds(c0, 256)]
            up = acc[rows(at, UNIT), pl.ds(c0 + HID, 256)]
            grad = acc[rows(at, UNIT), pl.ds(c0 + 2 * HID, 256)]
            sig = jax.nn.sigmoid(gate)
            act = gate * sig
            slope = sig * (1.0 + gate * (1.0 - sig))
            hb[out, pl.ds(c0, 256)] = (act * up).astype(BF16)
            hb[out, pl.ds(c0 + HID, 256)] = (grad * up * slope).astype(BF16)
            hb[out, pl.ds(c0 + 2 * HID, 256)] = (grad * act).astype(BF16)

        @pl.when(z < 3)
        def _():
            ag_copy(k, 0, z).start()

        @pl.when(z > 0)
        def _():
            ag_copy(k, 1, z).start()

        ag_copy(k, 2, z).start()

    def stage_a(k):
        for dist in (1, 2, 3):
            from_left = z - dist
            from_right = z + dist

            @pl.when(from_left >= 0)
            def _():
                ag_copy(k, 0, from_left).wait_recv()

                @pl.when(z < 3)
                def _():
                    ag_copy(k, 0, from_left).start()

                ag_copy(k, 2, from_left).start()

            @pl.when(from_right <= 3)
            def _():
                ag_copy(k, 1, from_right).wait_recv()

                @pl.when(z > 0)
                def _():
                    ag_copy(k, 1, from_right).start()

                ag_copy(k, 2, from_right).start()

    def stage_g(k):
        for j in range(4):
            part = rows(k * CHUNK + (1 - core) * SHARE + j * UNIT, UNIT)
            remote(
                hb.at[part], hb.at[part], ag_s.at[k, 2, j], ag_r.at[k, 1 - core, j], core_partner
            ).wait_recv()
        here = pl.ds(k * CHUNK, CHUNK)
        for c0, size in ((0, 256), (256, 256), (512, 256), (768, 128)):
            rowg[here, c0 : c0 + size] = mm(hb[here, HID:], wgu[c0 : c0 + size, :], NT).astype(BF16)
        if k < 2:

            @pl.loop(0, 16)
            def _(p):
                at = lax.rem(q + p, 16)
                to = (at // 8) * HALF + k * 8 + lax.rem(at, 8)

                @pl.when(to != me_e)
                def _():
                    remote(
                        rowg.at[rows(k * CHUNK + at * CAP, CAP)], back.at[rows(me_e * CAP, CAP)],
                        ret_s, ret_r, {"exp": to},
                    ).start()

                @pl.when(to == me_e)
                def _():
                    back[rows(me_e * CAP, CAP), :] = rowg[rows(k * CHUNK + at * CAP, CAP), :]
        else:

            @pl.loop(0, 8)
            def _(p):
                at = lax.rem(q + p, 8)
                near = (k - 2) * 8 + at
                src = rows(k * CHUNK + at * 2 * CAP, 2 * CAP)

                @pl.when(near != q)
                def _():
                    remote(
                        rowg.at[src], backo.at[rows(q * 2 * CAP, 2 * CAP)],
                        reto_s, reto_r, {"exp": half * HALF + near},
                    ).start()

                @pl.when(near == q)
                def _():
                    backo[rows(q * 2 * CAP, 2 * CAP), :] = rowg[src, :]

    def hot_rows():
        many(xin, (HALF - 1) * 2 * CAP, ov_send.at[0], ov_recv.at[0]).wait_recv()
        many(din, (HALF - 1) * 2 * CAP, ov_send.at[1], ov_recv.at[1]).wait_recv()

        @pl.loop(0, BASE // 16)
        def _(n):
            at = rows(BASE + n * 16, 16)
            xin[at, :] = xin[at, :] * hotm[...]
            din[at, :] = din[at, :] * hotm[...]

    stage_p(0)
    stage_c(0)
    stage_e(0)
    stage_p(1)
    stage_c(1)
    stage_m(0)
    stage_e(1)
    stage_f(0)
    hot_rows()
    stage_p(2)
    stage_c(2)
    stage_m(1)
    stage_e(2)
    stage_a(0)
    stage_f(1)
    stage_p(3)
    stage_c(3)
    stage_g(0)
    stage_m(2)
    stage_e(3)
    stage_a(1)
    stage_f(2)
    stage_g(1)
    stage_m(3)
    stage_a(2)
    stage_f(3)
    stage_g(2)
    stage_a(3)
    stage_g(3)

    def gate_up_grads():
        @pl.loop(0, 2 * HID // TILE)
        def _(n):
            c0 = pl.multiple_of(n * TILE, TILE)
            for f0, size in ((0, 256), (256, 256), (512, 256), (768, 128)):
                gug_ref[f0 : f0 + size, pl.ds(c0, TILE)] = mm(
                    xin[:, f0 : f0 + size], hb[:, pl.ds(c0 + HID, TILE)], TN
                ).astype(BF16)

    def down_grads():
        @pl.loop(0, HID // 256)
        def _(n):
            c0 = pl.multiple_of(n * 256, 256)
            dg_ref[pl.ds(c0, 256), :] = mm(hb[:, pl.ds(c0, 256)], din[...], TN).astype(BF16)

    down_grads()
    many(backo, (HALF - 1) * 2 * CAP, reto_s, reto_r).wait_recv()
    for c0 in (0, CAP):
        total = jnp.zeros((CAP, FEAT), F32)
        for n in range(HALF):
            total = total + backo[n * 2 * CAP + c0 : n * 2 * CAP + c0 + CAP, :].astype(F32)
        if c0:
            zsend[...] = total.astype(BF16)
        else:
            ovx_total = total
    back_z = remote(zsend, zrecv, retz_s, retz_r, z_partner)
    back_z.start()
    gate_up_grads()
    many(back, BASE - CAP, ret_s, ret_r).wait_recv()
    back_z.wait_recv()
    over_rows = (ovx_total + zrecv[...].astype(F32)).astype(BF16)
    over_at = picks(0.0, CAP, slots[1:2, :])
    total = mm(over_at, over_rows, TN)
    for b in range(BASE // 128):
        pick = picks(128.0 * b, 128, slots[0:1, :])
        total = total + mm(pick, back[b * 128 : (b + 1) * 128, :], TN)
    tg_ref[...] = total.astype(BF16)

    for copy in ovz:
        copy.wait_send()
    for n in range(2):
        many(sendx, BASE - CAP, base_send.at[n], base_recv.at[n]).wait_send()
        many(xin, (HALF - 1) * 2 * CAP, ov_send.at[n], ov_recv.at[n]).wait_send()
    many(rowg, BASE - CAP, ret_s, ret_r).wait_send()
    many(rowg, (HALF - 1) * 2 * CAP, reto_s, reto_r).wait_send()
    back_z.wait_send()
    for k in range(CHUNKS):
        core_copy(k).wait_send()
        for d in range(4):

            @pl.when(z < d)
            def _():
                rs_copy(k, 0, d).wait_send()

            @pl.when(z > d)
            def _():
                rs_copy(k, 1, d).wait_send()

            @pl.when(jnp.logical_and(z >= d, z < 3))
            def _():
                ag_copy(k, 0, d).wait_send()

            @pl.when(jnp.logical_and(z <= d, z > 0))
            def _():
                ag_copy(k, 1, d).wait_send()

            ag_copy(k, 2, d).wait_send()


def local(tokens, d_out, row_expert, w_gate_up, w_down):
    vmem = pl.BlockSpec(memory_space=pltpu.VMEM)
    hbm = pl.BlockSpec(memory_space=pl.ANY)
    dma = pltpu.SemaphoreType.DMA

    def buf(count, width, kind=BF16):
        return pltpu.VMEM((count, width), kind)

    token_grads, gate_up_grads, down_grads = pl.pallas_call(
        kernel,
        out_shape=(
            jax.ShapeDtypeStruct((ROWS, FEAT), BF16),
            jax.ShapeDtypeStruct((FEAT, 2 * HID), BF16),
            jax.ShapeDtypeStruct((HID, FEAT), BF16),
        ),
        in_specs=[vmem, vmem, vmem, hbm, hbm],
        out_specs=(vmem, vmem, vmem),
        scratch_shapes=[
            buf(FEAT, 2 * HID), buf(HID, FEAT),
            buf(SLOTS, FEAT), buf(SLOTS, FEAT),
            buf(BASE, FEAT), buf(BASE, FEAT),
            buf(2 * CAP, FEAT), buf(2 * CAP, FEAT),
            buf(SLOTS // 2, WIDE), buf(SLOTS // 2, WIDE),
            buf(SLOTS // 2, WIDE, F32),
            buf(CHUNKS * 8 * UNIT, WIDE), buf(CHUNKS * 8 * UNIT, WIDE),
            buf(SLOTS, WIDE),
            buf(SLOTS, FEAT), buf(BASE, FEAT), buf(BASE, FEAT),
            buf(CAP, FEAT), buf(CAP, FEAT),
            buf(8, ROWS, F32), buf(16, FEAT),
            dma((2,)), dma((2,)), dma((2,)), dma((2,)), dma((2,)), dma((2,)), dma((2,)),
            dma((CHUNKS,)), dma((CHUNKS,)),
            dma((CHUNKS, 2, 4)), dma((CHUNKS, 2, 4)),
            dma((CHUNKS, 3, 4)), dma((CHUNKS, 2, 4)),
            dma, dma, dma, dma, dma, dma,
        ],
        compiler_params=pltpu.CompilerParams(
            collective_id=0, has_side_effects=True, vmem_limit_bytes=62 * 1024 * 1024
        ),
        cost_estimate=pl.CostEstimate(flops=15_000_000_000, bytes_accessed=14_000_000, transcendentals=131072),
        name="expert_backward",
    )(
        row_expert.reshape(1, ROWS), tokens, d_out,
        w_gate_up.reshape(FEAT, 2 * HID), w_down.reshape(HID, FEAT),
    )
    return (
        token_grads,
        gate_up_grads.reshape(1, FEAT, 2, HID),
        down_grads.reshape(1, HID, FEAT),
    )


def solution(mesh):
    return jax.shard_map(
        local,
        mesh=mesh,
        in_specs=(
            P("exp", "grp"),
            P("exp", "grp"),
            P("exp"),
            P("exp", "grp", None, None),
            P("exp", None, "grp"),
        ),
        out_specs=(P("exp", "grp"), P("exp", "grp", None, None), P("exp", None, "grp")),
        check_vma=False,
    )
```

```python
import jax
import jax.numpy as jnp
from jax import lax
from jax.experimental import pallas as pl
from jax.experimental.pallas import tpu as pltpu
from jax.sharding import PartitionSpec as P

MESH = pl.DeviceIdType.MESH
F32 = jnp.float32
BF16 = jnp.bfloat16

ROWS = 256
FEAT = 896
HID = 1024
WIDE = 3 * HID
N_EXP = 32
HALF = 16
CAP = 16
BASE = N_EXP * CAP
SLOTS = 2 * BASE
GROUPS = 4
CHUNK = BASE // GROUPS
SHARE = CHUNK // 2
QUARTER = 64
UNIT = 16
TILE = 512
RINGS = 6

NN = (((1,), (0,)), ((), ()))
NT = (((1,), (1,)), ((), ()))
TN = (((0,), (0,)), ((), ()))


def mm(a, b, dims=NN):
    return lax.dot_general(a, b, dims, preferred_element_type=F32)


def rows(start, size):
    return pl.ds(pl.multiple_of(start, 16), size)


def kernel(
    expert_ref, tok_ref, dout_ref, wgu_hbm, wd_hbm,
    tg_ref, gug_hbm, dg_hbm,
    paired, down, wgu, wd, xin, din, sendx, sendd, ovx, ovd,
    csend, crecv, acc, rs_send, rs_recv, hb,
    ocsend, ocrecv, oacc, oxsend, oxrecv, ors_send, ors_recv, hbo,
    rowg, back, backo, zsend, zrecv, slots, hotm,
    w_sem, o_sem, base_send, base_recv, ovz_send, ovz_recv, ov_send, ov_recv,
    c_send, c_recv, x_send, x_recv, y_send, y_recv, yc_send, yc_recv,
    rs_s, rs_r, ag_s, ag_r, ret_s, ret_r, reto_s, reto_r, retz_s, retz_r,
):
    me_e = lax.axis_index("exp")
    me_g = lax.axis_index("grp")
    z = me_g // 2
    core = lax.rem(me_g, 2)
    half = me_e // HALF
    q = lax.rem(me_e, HALF)
    z_partner = {"exp": lax.rem(me_e + HALF, N_EXP)}
    core_partner = {"grp": me_g + 1 - 2 * core}
    x = lax.rem(me_e, 4)
    to_right = {"grp": lax.rem(me_g + 2, 8)}
    to_left = {"grp": lax.rem(me_g + 6, 8)}

    def remote(src, dst, s_sem, r_sem, dev):
        return pltpu.make_async_remote_copy(
            src_ref=src, dst_ref=dst, send_sem=s_sem, recv_sem=r_sem, device_id=dev, device_id_type=MESH
        )

    def peer(p, way):
        side = lax.rem(p // 4, 2)
        return lax.rem(half + side, 2) * HALF + lax.rem(q + HALF + way * ((p // 8) * 4 + lax.rem(p, 4)), HALF)

    w1 = pltpu.make_async_copy(wgu_hbm, paired, w_sem.at[0])
    w2 = pltpu.make_async_copy(wd_hbm, wd, w_sem.at[1])
    w1.start()
    w2.start()
    barrier = pltpu.get_barrier_semaphore()

    @pl.loop(1, N_EXP)
    def _(p):
        pl.semaphore_signal(
            barrier, inc=1, device_id={"exp": lax.rem(me_e + p, N_EXP)}, device_id_type=MESH
        )

    @pl.loop(1, 8)
    def _(p):
        pl.semaphore_signal(barrier, inc=1, device_id={"grp": lax.rem(me_g + p, 8)}, device_id_type=MESH)

    expert = expert_ref[...]
    e_iota = lax.broadcasted_iota(jnp.int32, (N_EXP, ROWS), 0)
    mine = (expert == e_iota).astype(F32)
    upto = (
        lax.broadcasted_iota(jnp.int32, (ROWS, ROWS), 0) <= lax.broadcasted_iota(jnp.int32, (ROWS, ROWS), 1)
    ).astype(F32).astype(BF16)
    running = mm(mine.astype(BF16), upto)
    rank = jnp.sum(running * mine, axis=0, keepdims=True) - 1.0
    slot = jnp.where(rank < CAP, expert.astype(F32) * CAP + rank, -1.0)
    over = rank - CAP
    slots[0:1, :] = slot
    slots[1:2, :] = over
    loads = jnp.sum(mine, axis=1, keepdims=True)
    is_me = (lax.broadcasted_iota(jnp.int32, (N_EXP, 1), 0) == me_e).astype(F32)
    hot = jnp.sum(jnp.where(loads > CAP + 0.5, 1.0, 0.0) * is_me, axis=0, keepdims=True)
    hotm[...] = jnp.broadcast_to(hot, (16, FEAT)).astype(BF16)

    def picks(start, size, values):
        at = lax.broadcasted_iota(jnp.int32, (size, ROWS), 0).astype(F32) + start
        return (at == values).astype(F32).astype(BF16)

    over_pick = picks(0.0, CAP, over)
    base_pick = picks(0.0, BASE, slot)
    for src, base, further in ((tok_ref, sendx, ovx), (dout_ref, sendd, ovd)):
        for c0, size in ((0, 256), (256, 256), (512, 256), (768, 128)):
            col = slice(c0, c0 + size)
            base[:, col] = mm(base_pick, src[:, col]).astype(BF16)
            further[0:CAP, col] = mm(over_pick, src[:, col]).astype(BF16)
    pl.semaphore_wait(barrier, N_EXP - 1 + 7)

    ovz = [
        remote(buf.at[pl.ds(0, CAP)], buf.at[pl.ds(CAP, CAP)], ovz_send.at[n], ovz_recv.at[n], z_partner)
        for n, buf in enumerate((ovx, ovd))
    ]
    for copy in ovz:
        copy.start()
    over_place = BASE + q * 2 * CAP

    def many(buf, count, s_sem, r_sem):
        part = buf.at[pl.ds(0, count)]
        return remote(part, part, s_sem, r_sem, z_partner)

    def base_block(k, p):
        to = peer(p, 1)
        for n, (src, dst) in enumerate(((sendx, xin), (sendd, din))):
            remote(
                src.at[rows(to * CAP, CAP)], dst.at[rows(p * CAP, CAP)],
                base_send.at[n, k], base_recv.at[n, k], {"exp": to},
            ).start()

    def further_block(first, p):
        to = half * HALF + lax.rem(q + p, HALF)
        for n, (src, dst) in enumerate(((ovx, xin), (ovd, din))):
            remote(
                src.at[pl.ds(first, CAP)], dst.at[rows(over_place + first, CAP)],
                ov_send.at[n], ov_recv.at[n], {"exp": to},
            ).start()

    def stage_d(k):
        @pl.loop(0, 8)
        def _(n):
            p = k * 8 + lax.rem(n + 4, 8)
            if k:
                base_block(k, p)
            else:

                @pl.when(p > 0)
                def _():
                    base_block(k, p)

            if k < 2:

                @pl.when(n > 0)
                def _():
                    further_block(k * CAP, 2 * n)

                further_block(k * CAP, 2 * n + 1)

    def left(k):
        for n, buf in enumerate((sendx, sendd)):
            many(buf, (8 if k else 7) * CAP, base_send.at[n, k], base_recv.at[n, k]).wait_send()

    stage_d(0)
    xin[0:CAP, :] = sendx[rows(me_e * CAP, CAP), :]
    din[0:CAP, :] = sendd[rows(me_e * CAP, CAP), :]
    w1.wait()

    @pl.loop(0, FEAT // 16)
    def _(n):
        at = rows(n * 16, 16)
        wgu[at, 0:HID] = paired[0, at, 0, :]
        wgu[at, HID:] = paired[0, at, 1, :]

    w2.wait()
    for copy in ovz:
        copy.wait_recv()
    stage_d(1)
    xin[rows(over_place, 2 * CAP), :] = ovx[...]
    din[rows(over_place, 2 * CAP), :] = ovd[...]

    def base_rows(k):
        for n, buf in enumerate((xin, din)):
            many(buf, (8 if k else 7) * CAP, base_send.at[n, k], base_recv.at[n, k]).wait_recv()

    def core_copy(n):
        src, dst = (csend, crecv) if n < GROUPS else (ocsend, ocrecv)
        part = pl.ds(n * SHARE, SHARE) if n < GROUPS else pl.ds((n - GROUPS) * 4 * QUARTER, 4 * QUARTER)
        return remote(src.at[part], dst.at[part], c_send.at[n], c_recv.at[n], core_partner)

    def stage_p(k):
        here = pl.ds(k * CHUNK, CHUNK)

        @pl.loop(0, 2 * HID // TILE)
        def _(n):
            col = pl.ds(pl.multiple_of(n * TILE, TILE), TILE)
            acc[here, col] = mm(xin[here, :], wgu[:, col])

        @pl.loop(0, HID // TILE)
        def _(n):
            col = pl.ds(pl.multiple_of(2 * HID + n * TILE, TILE), TILE)
            acc[here, col] = mm(din[here, :], wd[rows(n * TILE, TILE), :], NT)

        @pl.loop(0, SHARE // 16)
        def _(n):
            theirs = rows(k * CHUNK + (1 - core) * SHARE + n * 16, 16)
            csend[rows(k * SHARE + n * 16, 16), :] = acc[theirs, :].astype(BF16)

        core_copy(k).start()

    def stage_c(k):
        core_copy(k).wait_recv()

        @pl.loop(0, SHARE // 16)
        def _(n):
            mine = rows(k * CHUNK + core * SHARE + n * 16, 16)
            acc[mine, :] += crecv[rows(k * SHARE + n * 16, 16), :].astype(F32)

    def stage_po(h):
        @pl.loop(0, BASE // 128)
        def _(n):
            rows_in = xin[rows(BASE + n * 128, 128), :]
            grads_in = din[rows(BASE + n * 128, 128), :]
            here = rows(h * BASE + n * 128, 128)
            oacc[here, 0:TILE] = mm(rows_in, wgu[:, h * TILE : (h + 1) * TILE])
            oacc[here, TILE : 2 * TILE] = mm(rows_in, wgu[:, HID + h * TILE : HID + (h + 1) * TILE])
            oacc[here, 2 * TILE :] = mm(grads_in, wd[h * TILE : (h + 1) * TILE, :], NT)

        @pl.loop(0, 4 * QUARTER // 16)
        def _(n):
            theirs = rows(h * BASE + (1 - core) * 4 * QUARTER + n * 16, 16)
            ocsend[rows(h * 4 * QUARTER + n * 16, 16), :] = oacc[theirs, :].astype(BF16)

        core_copy(GROUPS + h).start()

    y = q // 4
    spot = (x, y)

    def along(h, p):
        return {"exp": me_e - x + lax.rem(x + p, 4) if h == 0 else me_e - 4 * y + 4 * lax.rem(y + p, 4)}

    def x_copy(h, p):
        return remote(
            oxsend.at[rows(h * 4 * QUARTER + lax.rem(spot[h] + p, 4) * QUARTER, QUARTER)],
            oxrecv.at[pl.ds((h * 3 + p - 1) * QUARTER, QUARTER)],
            x_send.at[h, p - 1], x_recv.at[h, p - 1], along(h, p),
        )

    def stage_co(h):
        core_copy(GROUPS + h).wait_recv()

        @pl.loop(0, 4 * QUARTER // 16)
        def _(n):
            mine = rows(h * BASE + core * 4 * QUARTER + n * 16, 16)
            here = rows(h * 4 * QUARTER + n * 16, 16)
            value = oacc[mine, :] + ocrecv[here, :].astype(F32)
            oacc[mine, :] = value
            oxsend[here, :] = value.astype(BF16)

        for p in (1, 2, 3):
            x_copy(h, p).start()

    def stage_xo(h):
        for p in (1, 2, 3):
            x_copy(h, p).wait_recv()

        @pl.loop(0, QUARTER // 16)
        def _(n):
            at = rows(h * BASE + further_row(spot[h], core) + n * 16, 16)
            value = oacc[at, :]
            for p in range(3):
                value = value + oxrecv[rows((h * 3 + p) * QUARTER + n * 16, 16), :].astype(F32)
            oacc[at, :] = value

    def ring(r):
        if r < GROUPS:
            return acc, rs_send, rs_recv, hb, r * 6, HID
        return oacc, ors_send, ors_recv, hbo, (r - GROUPS) * 6, TILE

    def block_row(r, c, j):
        if r < GROUPS:
            return r * CHUNK + c * SHARE + j * UNIT
        return (r - GROUPS) * BASE + further_row(spot[r - GROUPS], c) + j * UNIT

    def further_row(at, c):
        return c * 4 * QUARTER + at * QUARTER

    def rs_copy(r, way, d):
        _, send, recv, _, first, _ = ring(r)
        part = rows((first + way * 3 + d - 1 + way) * UNIT, UNIT)
        return remote(send.at[part], recv.at[part], rs_s.at[r, way, d], rs_r.at[r, way, d], (to_right, to_left)[way])

    def rs_forward(r, way, d, start):
        total, send, recv, _, first, _ = ring(r)
        part = pl.ds((first + way * 3 + d - 1 + way) * UNIT, UNIT)
        copy = rs_copy(r, way, d)
        value = total[rows(block_row(r, core, d), UNIT), :]
        if not start:
            copy.wait_recv()
            value = value + recv[part, :].astype(F32)
        send[part, :] = value.astype(BF16)
        copy.start()

    def stage_e(r):
        @pl.when(z == 0)
        def _():
            for d in (3, 2, 1):
                rs_forward(r, 0, d, True)

        @pl.when(z == 3)
        def _():
            for d in (0, 1, 2):
                rs_forward(r, 1, d, True)

    def stage_m1(r):
        @pl.when(z == 1)
        def _():
            rs_forward(r, 0, 3, False)

        @pl.when(z == 2)
        def _():
            rs_forward(r, 1, 0, False)

    def stage_m2(r):
        @pl.when(z == 1)
        def _():
            rs_forward(r, 0, 2, False)
            rs_forward(r, 1, 0, False)

        @pl.when(z == 2)
        def _():
            rs_forward(r, 1, 1, False)
            rs_forward(r, 0, 3, False)

    def ag_copy(r, way, j):
        out = ring(r)[3]
        part = rows(block_row(r, core, j), UNIT)
        return remote(
            out.at[part], out.at[part], ag_s.at[r, way, j], ag_r.at[r, core, j], (to_right, to_left, core_partner)[way]
        )

    def stage_f(r):
        total, _, recv, out, first, wide = ring(r)
        at = rows(block_row(r, core, z), UNIT)

        def fold(way):
            rs_copy(r, way, z).wait_recv()
            total[at, :] += recv[rows((first + way * 3 + z - 1 + way) * UNIT, UNIT), :].astype(F32)

        @pl.when(z > 0)
        def _():
            fold(0)

        @pl.when(z < 3)
        def _():
            fold(1)

        @pl.loop(0, wide // 256)
        def _(n):
            c0 = pl.multiple_of(n * 256, 256)
            gate = total[at, pl.ds(c0, 256)]
            up = total[at, pl.ds(c0 + wide, 256)]
            grad = total[at, pl.ds(c0 + 2 * wide, 256)]
            sig = jax.nn.sigmoid(gate)
            act = gate * sig
            slope = sig * (1.0 + gate * (1.0 - sig))
            out[at, pl.ds(c0, 256)] = (act * up).astype(BF16)
            out[at, pl.ds(c0 + wide, 256)] = (grad * up * slope).astype(BF16)
            out[at, pl.ds(c0 + 2 * wide, 256)] = (grad * act).astype(BF16)

        @pl.when(z < 3)
        def _():
            ag_copy(r, 0, z).start()

        @pl.when(z > 0)
        def _():
            ag_copy(r, 1, z).start()

        ag_copy(r, 2, z).start()

    def stage_a(r, dist):
        from_left = z - dist
        from_right = z + dist

        @pl.when(from_left >= 0)
        def _():
            ag_copy(r, 0, from_left).wait_recv()

            @pl.when(z < 3)
            def _():
                ag_copy(r, 0, from_left).start()

            ag_copy(r, 2, from_left).start()

        @pl.when(from_right <= 3)
        def _():
            ag_copy(r, 1, from_right).wait_recv()

            @pl.when(z > 0)
            def _():
                ag_copy(r, 1, from_right).start()

            ag_copy(r, 2, from_right).start()

    def y_copy(h, p):
        part = rows(h * BASE + further_row(spot[h], core), QUARTER)
        return remote(hbo.at[part], hbo.at[part], y_send.at[h, p - 1], y_recv.at[h, p - 1], along(h, p))

    def yc_copy(h, p, c):
        part = rows(h * BASE + further_row(lax.rem(spot[h] + 4 - p, 4), c), QUARTER)
        return remote(hbo.at[part], hbo.at[part], yc_send.at[h, p - 1], yc_recv.at[h, p - 1], core_partner)

    def stage_z(h):
        for p in (1, 2, 3):
            y_copy(h, p).start()

    def stage_y(h):
        for p in (1, 2, 3):
            y_copy(h, p).wait_recv()
            yc_copy(h, p, core).start()

    def from_core(r):
        out = ring(r)[3]
        for j in range(4):
            part = rows(block_row(r, 1 - core, j), UNIT)
            remote(
                out.at[part], out.at[part], ag_s.at[r, 2, j], ag_r.at[r, 1 - core, j], core_partner
            ).wait_recv()

    def stage_g(k):
        from_core(k)
        here = pl.ds(k * CHUNK, CHUNK)
        for c0, size in ((0, 256), (256, 256), (512, 256), (768, 128)):
            rowg[here, c0 : c0 + size] = mm(hb[here, HID:], wgu[c0 : c0 + size, :], NT).astype(BF16)

        @pl.loop(k * 8 if k else 1, k * 8 + 8)
        def _(p):
            to = peer(p, -1)
            remote(
                rowg.at[rows(p * CAP, CAP)], back.at[rows(me_e * CAP, CAP)], ret_s, ret_r, {"exp": to}
            ).start()

        if k == 0:
            back[rows(me_e * CAP, CAP), :] = rowg[0:CAP, :]

    def stage_go():
        for h in range(2):
            from_core(GROUPS + h)
            for p in (1, 2, 3):
                yc_copy(h, p, 1 - core).wait_recv()

        @pl.loop(0, 2)
        def _(n):
            for c0, size in ((0, 256), (256, 256), (512, 256), (768, 128)):
                value = jnp.zeros((256, size), F32)
                for h in range(2):
                    for b in range(2):
                        value = value + mm(
                            hbo[rows(h * BASE + n * 256, 256), (1 + b) * TILE : (2 + b) * TILE],
                            wgu[c0 : c0 + size, b * HID + h * TILE : b * HID + (h + 1) * TILE], NT,
                        )
                value = value * hotm[0:1, c0 : c0 + size].astype(F32)
                rowg[rows(BASE + n * 256, 256), c0 : c0 + size] = value.astype(BF16)

            @pl.loop(0, 8)
            def _(p):
                near = n * 8 + lax.rem(q + p, 8)

                @pl.when(near != q)
                def _():
                    remote(
                        rowg.at[rows(BASE + near * 2 * CAP, 2 * CAP)], backo.at[rows(q * 2 * CAP, 2 * CAP)],
                        reto_s, reto_r, {"exp": half * HALF + near},
                    ).start()

        backo[rows(q * 2 * CAP, 2 * CAP), :] = rowg[rows(BASE + q * 2 * CAP, 2 * CAP), :]

    def hot_rows():
        many(xin, (HALF - 1) * 2 * CAP, ov_send.at[0], ov_recv.at[0]).wait_recv()
        many(din, (HALF - 1) * 2 * CAP, ov_send.at[1], ov_recv.at[1]).wait_recv()

        @pl.loop(0, BASE // 16)
        def _(n):
            at = rows(BASE + n * 16, 16)
            xin[at, :] = xin[at, :] * hotm[...]
            din[at, :] = din[at, :] * hotm[...]

    left(0)
    stage_d(2)
    base_rows(0)
    stage_p(0)
    left(1)
    stage_d(3)
    base_rows(1)
    stage_p(1)
    hot_rows()
    stage_po(0)
    stage_po(1)
    stage_c(0)
    stage_e(0)
    stage_c(1)
    stage_e(1)
    stage_co(0)
    stage_co(1)
    stage_m1(0)
    stage_m1(1)
    stage_m2(0)
    stage_m2(1)
    stage_f(0)
    stage_f(1)
    base_rows(2)
    stage_p(2)
    stage_c(2)
    stage_xo(0)
    stage_xo(1)
    stage_e(4)
    stage_e(5)
    stage_a(0, 1)
    stage_a(1, 1)
    stage_m1(4)
    stage_m1(5)
    stage_a(0, 2)
    stage_a(1, 2)
    stage_m2(4)
    stage_m2(5)
    stage_a(0, 3)
    stage_a(1, 3)
    stage_f(4)
    stage_f(5)
    base_rows(3)
    stage_p(3)
    stage_c(3)
    stage_e(2)
    stage_e(3)
    stage_a(4, 1)
    stage_a(5, 1)
    stage_m1(2)
    stage_m1(3)
    stage_a(4, 2)
    stage_a(5, 2)
    stage_m2(2)
    stage_m2(3)
    stage_a(4, 3)
    stage_z(0)
    stage_a(5, 3)
    stage_z(1)
    stage_f(2)
    stage_f(3)
    stage_g(0)
    stage_g(1)
    stage_a(2, 1)
    stage_a(3, 1)
    stage_a(2, 2)
    stage_a(3, 2)
    stage_a(2, 3)
    stage_a(3, 3)
    stage_y(0)
    stage_y(1)
    stage_go()
    stage_g(2)
    stage_g(3)

    def gate_up_grads():
        for b in range(2):

            @pl.loop(0, HID // TILE)
            def _(n):
                c0 = pl.multiple_of(n * TILE, TILE)
                near = hb[:, pl.ds(c0 + HID * (1 + b), TILE)]
                further = hbo[rows(n * BASE, BASE), (1 + b) * TILE : (2 + b) * TILE]
                for f0, size in ((0, 256), (256, 256), (512, 256), (768, 128)):
                    value = mm(xin[0:BASE, f0 : f0 + size], near, TN)
                    value = value + mm(xin[BASE:, f0 : f0 + size], further, TN)
                    paired[0, f0 : f0 + size, b, pl.ds(c0, TILE)] = value.astype(BF16)

    def down_grads():
        for h in range(2):

            @pl.loop(0, 2)
            def _(n):
                c0 = pl.multiple_of(n * 256, 256)
                value = mm(hb[:, pl.ds(c0 + h * TILE, 256)], din[0:BASE, :], TN)
                value = value + mm(hbo[h * BASE : (h + 1) * BASE, pl.ds(c0, 256)], din[BASE:, :], TN)
                down[pl.ds(c0 + h * TILE, 256), :] = value.astype(BF16)

    out_down = pltpu.make_async_copy(down, dg_hbm, o_sem.at[0])
    out_gate_up = pltpu.make_async_copy(paired, gug_hbm, o_sem.at[1])
    gate_up_grads()
    out_gate_up.start()
    many(backo, (HALF - 1) * 2 * CAP, reto_s, reto_r).wait_recv()
    for c0 in (0, CAP):
        total = jnp.zeros((CAP, FEAT), F32)
        for n in range(HALF):
            total = total + backo[n * 2 * CAP + c0 : n * 2 * CAP + c0 + CAP, :].astype(F32)
        if c0:
            zsend[...] = total.astype(BF16)
        else:
            ovx_total = total
    back_z = remote(zsend, zrecv, retz_s, retz_r, z_partner)
    back_z.start()
    down_grads()
    out_down.start()
    many(back, BASE - CAP, ret_s, ret_r).wait_recv()
    back_z.wait_recv()
    over_rows = (ovx_total + zrecv[...].astype(F32)).astype(BF16)
    over_at = picks(0.0, CAP, slots[1:2, :])
    total = mm(over_at, over_rows, TN)
    for b in range(BASE // 128):
        pick = picks(128.0 * b, 128, slots[0:1, :])
        total = total + mm(pick, back[b * 128 : (b + 1) * 128, :], TN)
    tg_ref[...] = total.astype(BF16)

    out_down.wait()
    out_gate_up.wait()
    for copy in ovz:
        copy.wait_send()
    left(2)
    left(3)
    for n in range(2):
        many(xin, (HALF - 1) * 2 * CAP, ov_send.at[n], ov_recv.at[n]).wait_send()
    many(rowg, BASE - CAP, ret_s, ret_r).wait_send()
    many(rowg, (HALF - 1) * 2 * CAP, reto_s, reto_r).wait_send()
    back_z.wait_send()
    for n in range(RINGS):
        core_copy(n).wait_send()
    for h in range(2):
        for p in (1, 2, 3):
            x_copy(h, p).wait_send()
            y_copy(h, p).wait_send()
            yc_copy(h, p, core).wait_send()
    for r in range(RINGS):
        for d in range(4):
            if d > 0:

                @pl.when(z < d)
                def _():
                    rs_copy(r, 0, d).wait_send()

            if d < 3:

                @pl.when(z > d)
                def _():
                    rs_copy(r, 1, d).wait_send()

            @pl.when(jnp.logical_and(z >= d, z < 3))
            def _():
                ag_copy(r, 0, d).wait_send()

            @pl.when(jnp.logical_and(z <= d, z > 0))
            def _():
                ag_copy(r, 1, d).wait_send()

            ag_copy(r, 2, d).wait_send()


def hand_over(tg, gug, dg, tg_out, gug_out, dg_out, tg_via, gug_via, dg_via, sems):
    parts = [(tg, tg_via, tg_out)]
    for n in range(2):
        part = pl.ds(n * (HID // 2), HID // 2)
        parts.append((dg.at[part], dg_via.at[part], dg_out.at[part]))
    for n in range(4):
        part = pl.ds(n * (FEAT // 4), FEAT // 4)
        parts.append((gug.at[0, part], gug_via.at[0, part], gug_out.at[0, part]))
    here = [pltpu.make_async_copy(a, b, sems.at[0, n]) for n, (a, b, _) in enumerate(parts)]
    there = [pltpu.make_async_copy(b, c, sems.at[1, n]) for n, (_, b, c) in enumerate(parts)]
    for copy in here:
        copy.start()
    for first, then in zip(here, there):
        first.wait()
        then.start()
    for copy in there:
        copy.wait()


def local(tokens, d_out, row_expert, w_gate_up, w_down):
    vmem = pl.BlockSpec(memory_space=pltpu.VMEM)
    hbm = pl.BlockSpec(memory_space=pl.ANY)
    dma = pltpu.SemaphoreType.DMA

    def buf(count, width, kind=BF16):
        return pltpu.VMEM((count, width), kind)

    token_grads, gate_up_grads, down_grads = pl.pallas_call(
        kernel,
        out_shape=(
            jax.ShapeDtypeStruct((ROWS, FEAT), BF16),
            jax.ShapeDtypeStruct((1, FEAT, 2, HID), BF16),
            jax.ShapeDtypeStruct((HID, FEAT), BF16),
        ),
        in_specs=[vmem, vmem, vmem, hbm, hbm],
        out_specs=(vmem, hbm, hbm),
        scratch_shapes=[
            pltpu.VMEM((1, FEAT, 2, HID), BF16), buf(HID, FEAT),
            buf(FEAT, 2 * HID), buf(HID, FEAT),
            buf(SLOTS, FEAT), buf(SLOTS, FEAT),
            buf(BASE, FEAT), buf(BASE, FEAT),
            buf(2 * CAP, FEAT), buf(2 * CAP, FEAT),
            buf(BASE // 2, WIDE), buf(BASE // 2, WIDE),
            buf(BASE, WIDE, F32),
            buf(GROUPS * 6 * UNIT, WIDE), buf(GROUPS * 6 * UNIT, WIDE),
            buf(BASE, WIDE),
            buf(8 * QUARTER, 3 * TILE), buf(8 * QUARTER, 3 * TILE),
            buf(2 * BASE, 3 * TILE, F32),
            buf(8 * QUARTER, 3 * TILE), buf(6 * QUARTER, 3 * TILE),
            buf(2 * 6 * UNIT, 3 * TILE), buf(2 * 6 * UNIT, 3 * TILE),
            buf(2 * BASE, 3 * TILE),
            buf(SLOTS, FEAT), buf(BASE, FEAT), buf(BASE, FEAT),
            buf(CAP, FEAT), buf(CAP, FEAT),
            buf(8, ROWS, F32), buf(16, FEAT),
            dma((2,)), dma((2,)), dma((2, GROUPS)), dma((2, GROUPS)), dma((2,)), dma((2,)), dma((2,)), dma((2,)),
            dma((RINGS,)), dma((RINGS,)),
            dma((2, 3)), dma((2, 3)), dma((2, 3)), dma((2, 3)), dma((2, 3)), dma((2, 3)),
            dma((RINGS, 2, 4)), dma((RINGS, 2, 4)),
            dma((RINGS, 3, 4)), dma((RINGS, 2, 4)),
            dma, dma, dma, dma, dma, dma,
        ],
        compiler_params=pltpu.CompilerParams(
            collective_id=0, has_side_effects=True, vmem_limit_bytes=62 * 1024 * 1024
        ),
        cost_estimate=pl.CostEstimate(flops=15_000_000_000, bytes_accessed=14_000_000, transcendentals=131072),
        name="expert_backward",
    )(
        row_expert.reshape(1, ROWS), tokens, d_out,
        w_gate_up, w_down.reshape(HID, FEAT),
    )
    grads = (token_grads, gate_up_grads, down_grads.reshape(HID, FEAT))
    token_grads, gate_up_grads, down_grads = pl.pallas_call(
        hand_over,
        out_shape=tuple(jax.ShapeDtypeStruct(g.shape, g.dtype) for g in grads),
        in_specs=[hbm] * 3,
        out_specs=(hbm,) * 3,
        scratch_shapes=[buf(ROWS, FEAT), pltpu.VMEM((1, FEAT, 2, HID), BF16), buf(HID, FEAT), dma((2, 7))],
        name="hand_over",
    )(*grads)
    return token_grads, gate_up_grads, down_grads.reshape(1, HID, FEAT)


def solution(mesh):
    return jax.shard_map(
        local,
        mesh=mesh,
        in_specs=(
            P("exp", "grp"),
            P("exp", "grp"),
            P("exp"),
            P("exp", "grp", None, None),
            P("exp", None, "grp"),
        ),
        out_specs=(P("exp", "grp"), P("exp", "grp", None, None), P("exp", None, "grp")),
        check_vma=False,
    )
```

```python
import jax
import jax.numpy as jnp
from jax import lax
from jax.experimental import pallas as pl
from jax.experimental.pallas import tpu as pltpu
from jax.sharding import PartitionSpec as P

MESH = pl.DeviceIdType.MESH
F32 = jnp.float32
BF16 = jnp.bfloat16

ROWS = 256
FEAT = 896
HID = 1024
WIDE = 3 * HID
N_EXP = 32
HALF = 16
CAP = 16
BASE = N_EXP * CAP
SLOTS = 2 * BASE
GROUPS = 4
CHUNK = BASE // GROUPS
SHARE = CHUNK // 2
QUARTER = 64
UNIT = 16
TILE = 512
RINGS = 6

NN = (((1,), (0,)), ((), ()))
NT = (((1,), (1,)), ((), ()))
TN = (((0,), (0,)), ((), ()))


def mm(a, b, dims=NN):
    return lax.dot_general(a, b, dims, preferred_element_type=F32)


def rows(start, size):
    return pl.ds(pl.multiple_of(start, 16), size)


def kernel(
    expert_ref, tok_ref, dout_ref, wgu_hbm, wd_hbm,
    tg_ref, gug_hbm, dg_hbm,
    paired, down, wgu, wd, xin, din, sendx, sendd, ovx, ovd,
    csend, crecv, acc, rs_send, rs_recv, hb,
    ocsend, ocrecv, oacc, oxsend, oxrecv, ors_send, ors_recv, hbo,
    rowg, back, backo, zsend, zrecv, slots, hotm,
    w_sem, o_sem, base_send, base_recv, ovz_send, ovz_recv, ov_send, ov_recv,
    c_send, c_recv, x_send, x_recv, y_send, y_recv, yc_send, yc_recv,
    rs_s, rs_r, ag_s, ag_r, ret_s, ret_r, reto_s, reto_r, retz_s, retz_r,
):
    me_e = lax.axis_index("exp")
    me_g = lax.axis_index("grp")
    z = me_g // 2
    core = lax.rem(me_g, 2)
    half = me_e // HALF
    q = lax.rem(me_e, HALF)
    z_partner = {"exp": lax.rem(me_e + HALF, N_EXP)}
    core_partner = {"grp": me_g + 1 - 2 * core}
    x = lax.rem(me_e, 4)
    to_right = {"grp": lax.rem(me_g + 2, 8)}
    to_left = {"grp": lax.rem(me_g + 6, 8)}

    def remote(src, dst, s_sem, r_sem, dev):
        return pltpu.make_async_remote_copy(
            src_ref=src, dst_ref=dst, send_sem=s_sem, recv_sem=r_sem, device_id=dev, device_id_type=MESH
        )

    def peer(p, way):
        side = lax.rem(p // 4, 2)
        return lax.rem(half + side, 2) * HALF + lax.rem(q + HALF + way * ((p // 8) * 4 + lax.rem(p, 4)), HALF)

    w1 = pltpu.make_async_copy(wgu_hbm, paired, w_sem.at[0])
    w2 = pltpu.make_async_copy(wd_hbm, wd, w_sem.at[1])
    w1.start()
    w2.start()
    barrier = pltpu.get_barrier_semaphore()

    @pl.loop(1, N_EXP)
    def _(p):
        pl.semaphore_signal(
            barrier, inc=1, device_id={"exp": lax.rem(me_e + p, N_EXP)}, device_id_type=MESH
        )

    @pl.loop(1, 8)
    def _(p):
        pl.semaphore_signal(barrier, inc=1, device_id={"grp": lax.rem(me_g + p, 8)}, device_id_type=MESH)

    expert = expert_ref[...]
    e_iota = lax.broadcasted_iota(jnp.int32, (N_EXP, ROWS), 0)
    mine = (expert == e_iota).astype(F32)
    upto = (
        lax.broadcasted_iota(jnp.int32, (ROWS, ROWS), 0) <= lax.broadcasted_iota(jnp.int32, (ROWS, ROWS), 1)
    ).astype(F32).astype(BF16)
    running = mm(mine.astype(BF16), upto)
    rank = jnp.sum(running * mine, axis=0, keepdims=True) - 1.0
    slot = jnp.where(rank < CAP, expert.astype(F32) * CAP + rank, -1.0)
    over = rank - CAP
    slots[0:1, :] = slot
    slots[1:2, :] = over
    loads = jnp.sum(mine, axis=1, keepdims=True)
    is_me = (lax.broadcasted_iota(jnp.int32, (N_EXP, 1), 0) == me_e).astype(F32)
    hot = jnp.sum(jnp.where(loads > CAP + 0.5, 1.0, 0.0) * is_me, axis=0, keepdims=True)
    hotm[...] = jnp.broadcast_to(hot, (16, FEAT)).astype(BF16)

    def picks(start, size, values):
        at = lax.broadcasted_iota(jnp.int32, (size, ROWS), 0).astype(F32) + start
        return (at == values).astype(F32).astype(BF16)

    over_pick = picks(0.0, CAP, over)
    base_pick = picks(0.0, BASE, slot)
    for src, base, further in ((tok_ref, sendx, ovx), (dout_ref, sendd, ovd)):
        for c0, size in ((0, 256), (256, 256), (512, 256), (768, 128)):
            col = slice(c0, c0 + size)
            base[:, col] = mm(base_pick, src[:, col]).astype(BF16)
            further[0:CAP, col] = mm(over_pick, src[:, col]).astype(BF16)
    pl.semaphore_wait(barrier, N_EXP - 1 + 7)

    ovz = [
        remote(buf.at[pl.ds(0, CAP)], buf.at[pl.ds(CAP, CAP)], ovz_send.at[n], ovz_recv.at[n], z_partner)
        for n, buf in enumerate((ovx, ovd))
    ]
    for copy in ovz:
        copy.start()
    over_place = BASE + q * 2 * CAP

    def many(buf, count, s_sem, r_sem):
        part = buf.at[pl.ds(0, count)]
        return remote(part, part, s_sem, r_sem, z_partner)

    def base_block(k, p):
        to = peer(p, 1)
        for n, (src, dst) in enumerate(((sendx, xin), (sendd, din))):
            remote(
                src.at[rows(to * CAP, CAP)], dst.at[rows(p * CAP, CAP)],
                base_send.at[n, k], base_recv.at[n, k], {"exp": to},
            ).start()

    def further_block(first, p):
        to = half * HALF + lax.rem(q + p, HALF)
        for n, (src, dst) in enumerate(((ovx, xin), (ovd, din))):
            remote(
                src.at[pl.ds(first, CAP)], dst.at[rows(over_place + first, CAP)],
                ov_send.at[n], ov_recv.at[n], {"exp": to},
            ).start()

    def stage_d(k):
        @pl.loop(0, 8)
        def _(n):
            p = k * 8 + lax.rem(n + 4, 8)
            if k:
                base_block(k, p)
            else:

                @pl.when(p > 0)
                def _():
                    base_block(k, p)


    def left(k):
        for n, buf in enumerate((sendx, sendd)):
            many(buf, (8 if k else 7) * CAP, base_send.at[n, k], base_recv.at[n, k]).wait_send()

    @pl.loop(1, HALF)
    def _(p):
        further_block(0, p)

    stage_d(0)
    xin[0:CAP, :] = sendx[rows(me_e * CAP, CAP), :]
    din[0:CAP, :] = sendd[rows(me_e * CAP, CAP), :]
    w1.wait()

    @pl.loop(0, FEAT // 16)
    def _(n):
        at = rows(n * 16, 16)
        wgu[at, 0:HID] = paired[0, at, 0, :]
        wgu[at, HID:] = paired[0, at, 1, :]

    w2.wait()
    for copy in ovz:
        copy.wait_recv()

    @pl.loop(1, HALF)
    def _(p):
        further_block(CAP, p)

    stage_d(1)
    xin[rows(over_place, 2 * CAP), :] = ovx[...]
    din[rows(over_place, 2 * CAP), :] = ovd[...]

    def base_rows(k):
        for n, buf in enumerate((xin, din)):
            many(buf, (8 if k else 7) * CAP, base_send.at[n, k], base_recv.at[n, k]).wait_recv()

    def core_copy(n):
        src, dst = (csend, crecv) if n < GROUPS else (ocsend, ocrecv)
        part = pl.ds(n * SHARE, SHARE) if n < GROUPS else pl.ds((n - GROUPS) * 4 * QUARTER, 4 * QUARTER)
        return remote(src.at[part], dst.at[part], c_send.at[n], c_recv.at[n], core_partner)

    def stage_p(k):
        here = pl.ds(k * CHUNK, CHUNK)

        @pl.loop(0, 2 * HID // TILE)
        def _(n):
            col = pl.ds(pl.multiple_of(n * TILE, TILE), TILE)
            acc[here, col] = mm(xin[here, :], wgu[:, col])

        @pl.loop(0, HID // TILE)
        def _(n):
            col = pl.ds(pl.multiple_of(2 * HID + n * TILE, TILE), TILE)
            acc[here, col] = mm(din[here, :], wd[rows(n * TILE, TILE), :], NT)

        @pl.loop(0, SHARE // 16)
        def _(n):
            theirs = rows(k * CHUNK + (1 - core) * SHARE + n * 16, 16)
            csend[rows(k * SHARE + n * 16, 16), :] = acc[theirs, :].astype(BF16)

        core_copy(k).start()

    def stage_c(k):
        core_copy(k).wait_recv()

        @pl.loop(0, SHARE // 16)
        def _(n):
            mine = rows(k * CHUNK + core * SHARE + n * 16, 16)
            acc[mine, :] += crecv[rows(k * SHARE + n * 16, 16), :].astype(F32)

    def stage_po(h):
        @pl.loop(0, BASE // 128)
        def _(n):
            rows_in = xin[rows(BASE + n * 128, 128), :]
            grads_in = din[rows(BASE + n * 128, 128), :]
            here = rows(h * BASE + n * 128, 128)
            oacc[here, 0:TILE] = mm(rows_in, wgu[:, h * TILE : (h + 1) * TILE])
            oacc[here, TILE : 2 * TILE] = mm(rows_in, wgu[:, HID + h * TILE : HID + (h + 1) * TILE])
            oacc[here, 2 * TILE :] = mm(grads_in, wd[h * TILE : (h + 1) * TILE, :], NT)

        @pl.loop(0, 4 * QUARTER // 16)
        def _(n):
            theirs = rows(h * BASE + (1 - core) * 4 * QUARTER + n * 16, 16)
            ocsend[rows(h * 4 * QUARTER + n * 16, 16), :] = oacc[theirs, :].astype(BF16)

        core_copy(GROUPS + h).start()

    y = q // 4
    spot = (x, y)

    def along(h, p):
        return {"exp": me_e - x + lax.rem(x + p, 4) if h == 0 else me_e - 4 * y + 4 * lax.rem(y + p, 4)}

    def x_copy(h, p):
        return remote(
            oxsend.at[rows(h * 4 * QUARTER + lax.rem(spot[h] + p, 4) * QUARTER, QUARTER)],
            oxrecv.at[pl.ds((h * 3 + p - 1) * QUARTER, QUARTER)],
            x_send.at[h, p - 1], x_recv.at[h, p - 1], along(h, p),
        )

    def stage_co(h):
        core_copy(GROUPS + h).wait_recv()

        @pl.loop(0, 4 * QUARTER // 16)
        def _(n):
            mine = rows(h * BASE + core * 4 * QUARTER + n * 16, 16)
            here = rows(h * 4 * QUARTER + n * 16, 16)
            value = oacc[mine, :] + ocrecv[here, :].astype(F32)
            oacc[mine, :] = value
            oxsend[here, :] = value.astype(BF16)

        for p in (1, 2, 3):
            x_copy(h, p).start()

    def stage_xo(h):
        for p in (1, 2, 3):
            x_copy(h, p).wait_recv()

        @pl.loop(0, QUARTER // 16)
        def _(n):
            at = rows(h * BASE + further_row(spot[h], core) + n * 16, 16)
            value = oacc[at, :]
            for p in range(3):
                value = value + oxrecv[rows((h * 3 + p) * QUARTER + n * 16, 16), :].astype(F32)
            oacc[at, :] = value

    def ring(r):
        if r < GROUPS:
            return acc, rs_send, rs_recv, hb, r * 6, HID
        return oacc, ors_send, ors_recv, hbo, (r - GROUPS) * 6, TILE

    def block_row(r, c, j):
        if r < GROUPS:
            return r * CHUNK + c * SHARE + j * UNIT
        return (r - GROUPS) * BASE + further_row(spot[r - GROUPS], c) + j * UNIT

    def further_row(at, c):
        return c * 4 * QUARTER + at * QUARTER

    def rs_copy(r, way, d):
        _, send, recv, _, first, _ = ring(r)
        part = rows((first + way * 3 + d - 1 + way) * UNIT, UNIT)
        return remote(send.at[part], recv.at[part], rs_s.at[r, way, d], rs_r.at[r, way, d], (to_right, to_left)[way])

    def rs_forward(r, way, d, start):
        total, send, recv, _, first, _ = ring(r)
        part = pl.ds((first + way * 3 + d - 1 + way) * UNIT, UNIT)
        copy = rs_copy(r, way, d)
        value = total[rows(block_row(r, core, d), UNIT), :]
        if not start:
            copy.wait_recv()
            value = value + recv[part, :].astype(F32)
        send[part, :] = value.astype(BF16)
        copy.start()

    def stage_e(r):
        @pl.when(z == 0)
        def _():
            for d in (3, 2, 1):
                rs_forward(r, 0, d, True)

        @pl.when(z == 3)
        def _():
            for d in (0, 1, 2):
                rs_forward(r, 1, d, True)

    def stage_m1(r):
        @pl.when(z == 1)
        def _():
            rs_forward(r, 0, 3, False)

        @pl.when(z == 2)
        def _():
            rs_forward(r, 1, 0, False)

    def stage_m2(r):
        @pl.when(z == 1)
        def _():
            rs_forward(r, 0, 2, False)
            rs_forward(r, 1, 0, False)

        @pl.when(z == 2)
        def _():
            rs_forward(r, 1, 1, False)
            rs_forward(r, 0, 3, False)

    def ag_copy(r, way, j):
        out = ring(r)[3]
        part = rows(block_row(r, core, j), UNIT)
        return remote(
            out.at[part], out.at[part], ag_s.at[r, way, j], ag_r.at[r, core, j], (to_right, to_left, core_partner)[way]
        )

    def stage_f(r):
        total, _, recv, out, first, wide = ring(r)
        at = rows(block_row(r, core, z), UNIT)

        def fold(way):
            rs_copy(r, way, z).wait_recv()
            total[at, :] += recv[rows((first + way * 3 + z - 1 + way) * UNIT, UNIT), :].astype(F32)

        @pl.when(z > 0)
        def _():
            fold(0)

        @pl.when(z < 3)
        def _():
            fold(1)

        @pl.loop(0, wide // 256)
        def _(n):
            c0 = pl.multiple_of(n * 256, 256)
            gate = total[at, pl.ds(c0, 256)]
            up = total[at, pl.ds(c0 + wide, 256)]
            grad = total[at, pl.ds(c0 + 2 * wide, 256)]
            sig = jax.nn.sigmoid(gate)
            act = gate * sig
            slope = sig * (1.0 + gate * (1.0 - sig))
            out[at, pl.ds(c0, 256)] = (act * up).astype(BF16)
            out[at, pl.ds(c0 + wide, 256)] = (grad * up * slope).astype(BF16)
            out[at, pl.ds(c0 + 2 * wide, 256)] = (grad * act).astype(BF16)

        @pl.when(z < 3)
        def _():
            ag_copy(r, 0, z).start()

        @pl.when(z > 0)
        def _():
            ag_copy(r, 1, z).start()

        ag_copy(r, 2, z).start()

    def stage_a(r, dist):
        from_left = z - dist
        from_right = z + dist

        @pl.when(from_left >= 0)
        def _():
            ag_copy(r, 0, from_left).wait_recv()

            @pl.when(z < 3)
            def _():
                ag_copy(r, 0, from_left).start()

            ag_copy(r, 2, from_left).start()

        @pl.when(from_right <= 3)
        def _():
            ag_copy(r, 1, from_right).wait_recv()

            @pl.when(z > 0)
            def _():
                ag_copy(r, 1, from_right).start()

            ag_copy(r, 2, from_right).start()

    def y_copy(h, p):
        part = rows(h * BASE + further_row(spot[h], core), QUARTER)
        return remote(hbo.at[part], hbo.at[part], y_send.at[h, p - 1], y_recv.at[h, p - 1], along(h, p))

    def yc_copy(h, p, c):
        part = rows(h * BASE + further_row(lax.rem(spot[h] + 4 - p, 4), c), QUARTER)
        return remote(hbo.at[part], hbo.at[part], yc_send.at[h, p - 1], yc_recv.at[h, p - 1], core_partner)

    def stage_z(h):
        for p in (1, 2, 3):
            y_copy(h, p).start()

    def stage_y(h):
        for p in (1, 2, 3):
            y_copy(h, p).wait_recv()
            yc_copy(h, p, core).start()

    def from_core(r):
        out = ring(r)[3]
        for j in range(4):
            part = rows(block_row(r, 1 - core, j), UNIT)
            remote(
                out.at[part], out.at[part], ag_s.at[r, 2, j], ag_r.at[r, 1 - core, j], core_partner
            ).wait_recv()

    def stage_g(k):
        from_core(k)
        here = pl.ds(k * CHUNK, CHUNK)
        for c0, size in ((0, 256), (256, 256), (512, 256), (768, 128)):
            rowg[here, c0 : c0 + size] = mm(hb[here, HID:], wgu[c0 : c0 + size, :], NT).astype(BF16)

        @pl.loop(k * 8 if k else 1, k * 8 + 8)
        def _(p):
            to = peer(p, -1)
            remote(
                rowg.at[rows(p * CAP, CAP)], back.at[rows(me_e * CAP, CAP)], ret_s, ret_r, {"exp": to}
            ).start()

        if k == 0:
            back[rows(me_e * CAP, CAP), :] = rowg[0:CAP, :]

    def stage_go():
        for h in range(2):
            from_core(GROUPS + h)
            for p in (1, 2, 3):
                yc_copy(h, p, 1 - core).wait_recv()

        @pl.loop(0, 2)
        def _(n):
            for c0, size in ((0, 256), (256, 256), (512, 256), (768, 128)):
                value = jnp.zeros((256, size), F32)
                for h in range(2):
                    for b in range(2):
                        value = value + mm(
                            hbo[rows(h * BASE + n * 256, 256), (1 + b) * TILE : (2 + b) * TILE],
                            wgu[c0 : c0 + size, b * HID + h * TILE : b * HID + (h + 1) * TILE], NT,
                        )
                value = value * hotm[0:1, c0 : c0 + size].astype(F32)
                rowg[rows(BASE + n * 256, 256), c0 : c0 + size] = value.astype(BF16)

            @pl.loop(0, 8)
            def _(p):
                near = n * 8 + lax.rem(q + p, 8)

                @pl.when(near != q)
                def _():
                    remote(
                        rowg.at[rows(BASE + near * 2 * CAP, 2 * CAP)], backo.at[rows(q * 2 * CAP, 2 * CAP)],
                        reto_s, reto_r, {"exp": half * HALF + near},
                    ).start()

        backo[rows(q * 2 * CAP, 2 * CAP), :] = rowg[rows(BASE + q * 2 * CAP, 2 * CAP), :]

    def hot_rows():
        many(xin, (HALF - 1) * 2 * CAP, ov_send.at[0], ov_recv.at[0]).wait_recv()
        many(din, (HALF - 1) * 2 * CAP, ov_send.at[1], ov_recv.at[1]).wait_recv()

        @pl.loop(0, BASE // 16)
        def _(n):
            at = rows(BASE + n * 16, 16)
            xin[at, :] = xin[at, :] * hotm[...]
            din[at, :] = din[at, :] * hotm[...]

    left(0)
    stage_d(2)
    base_rows(0)
    stage_p(0)
    stage_c(0)
    stage_e(0)
    left(1)
    stage_d(3)
    base_rows(1)
    stage_p(1)
    stage_c(1)
    stage_e(1)
    hot_rows()
    stage_po(0)
    stage_m1(0)
    stage_po(1)
    stage_m1(1)
    stage_co(0)
    stage_co(1)
    stage_m2(0)
    stage_m2(1)
    stage_f(0)
    stage_f(1)
    base_rows(2)
    stage_p(2)
    stage_c(2)
    base_rows(3)
    stage_p(3)
    stage_c(3)
    stage_xo(0)
    stage_xo(1)
    stage_e(4)
    stage_e(5)
    stage_a(0, 1)
    stage_a(1, 1)
    stage_m1(4)
    stage_m1(5)
    stage_a(0, 2)
    stage_a(1, 2)
    stage_m2(4)
    stage_m2(5)
    stage_e(2)
    stage_e(3)
    stage_a(0, 3)
    stage_a(1, 3)
    stage_f(4)
    stage_f(5)
    stage_m1(2)
    stage_m1(3)
    stage_a(4, 1)
    stage_a(5, 1)
    stage_a(4, 2)
    stage_a(5, 2)
    stage_m2(2)
    stage_m2(3)
    stage_a(4, 3)
    stage_z(0)
    stage_a(5, 3)
    stage_z(1)
    stage_f(2)
    stage_f(3)
    stage_g(0)
    stage_a(2, 1)
    stage_a(3, 1)
    stage_y(0)
    stage_y(1)
    stage_go()
    stage_a(2, 2)
    stage_a(3, 2)
    stage_g(1)
    stage_a(2, 3)
    stage_a(3, 3)
    stage_g(2)
    stage_g(3)

    def gate_up_grads():
        for b in range(2):

            @pl.loop(0, HID // TILE)
            def _(n):
                c0 = pl.multiple_of(n * TILE, TILE)
                near = hb[:, pl.ds(c0 + HID * (1 + b), TILE)]
                further = hbo[rows(n * BASE, BASE), (1 + b) * TILE : (2 + b) * TILE]
                for f0, size in ((0, 256), (256, 256), (512, 256), (768, 128)):
                    value = mm(xin[0:BASE, f0 : f0 + size], near, TN)
                    value = value + mm(xin[BASE:, f0 : f0 + size], further, TN)
                    paired[0, f0 : f0 + size, b, pl.ds(c0, TILE)] = value.astype(BF16)

    def down_grads():
        for h in range(2):

            @pl.loop(0, 2)
            def _(n):
                c0 = pl.multiple_of(n * 256, 256)
                value = mm(hb[:, pl.ds(c0 + h * TILE, 256)], din[0:BASE, :], TN)
                value = value + mm(hbo[h * BASE : (h + 1) * BASE, pl.ds(c0, 256)], din[BASE:, :], TN)
                down[pl.ds(c0 + h * TILE, 256), :] = value.astype(BF16)

    out_down = pltpu.make_async_copy(down, dg_hbm, o_sem.at[0])
    out_gate_up = pltpu.make_async_copy(paired, gug_hbm, o_sem.at[1])
    gate_up_grads()
    out_gate_up.start()
    many(backo, (HALF - 1) * 2 * CAP, reto_s, reto_r).wait_recv()
    for c0 in (0, CAP):
        total = jnp.zeros((CAP, FEAT), F32)
        for n in range(HALF):
            total = total + backo[n * 2 * CAP + c0 : n * 2 * CAP + c0 + CAP, :].astype(F32)
        if c0:
            zsend[...] = total.astype(BF16)
        else:
            ovx_total = total
    back_z = remote(zsend, zrecv, retz_s, retz_r, z_partner)
    back_z.start()
    down_grads()
    out_down.start()
    many(back, BASE - CAP, ret_s, ret_r).wait_recv()
    back_z.wait_recv()
    over_rows = (ovx_total + zrecv[...].astype(F32)).astype(BF16)
    over_at = picks(0.0, CAP, slots[1:2, :])
    total = mm(over_at, over_rows, TN)
    for b in range(BASE // 128):
        pick = picks(128.0 * b, 128, slots[0:1, :])
        total = total + mm(pick, back[b * 128 : (b + 1) * 128, :], TN)
    tg_ref[...] = total.astype(BF16)

    out_down.wait()
    out_gate_up.wait()
    for copy in ovz:
        copy.wait_send()
    left(2)
    left(3)
    for n in range(2):
        many(xin, (HALF - 1) * 2 * CAP, ov_send.at[n], ov_recv.at[n]).wait_send()
    many(rowg, BASE - CAP, ret_s, ret_r).wait_send()
    many(rowg, (HALF - 1) * 2 * CAP, reto_s, reto_r).wait_send()
    back_z.wait_send()
    for n in range(RINGS):
        core_copy(n).wait_send()
    for h in range(2):
        for p in (1, 2, 3):
            x_copy(h, p).wait_send()
            y_copy(h, p).wait_send()
            yc_copy(h, p, core).wait_send()
    for r in range(RINGS):
        for d in range(4):
            if d > 0:

                @pl.when(z < d)
                def _():
                    rs_copy(r, 0, d).wait_send()

            if d < 3:

                @pl.when(z > d)
                def _():
                    rs_copy(r, 1, d).wait_send()

            @pl.when(jnp.logical_and(z >= d, z < 3))
            def _():
                ag_copy(r, 0, d).wait_send()

            @pl.when(jnp.logical_and(z <= d, z > 0))
            def _():
                ag_copy(r, 1, d).wait_send()

            ag_copy(r, 2, d).wait_send()


def hand_over(tg, gug, dg, tg_out, gug_out, dg_out, tg_via, gug_via, dg_via, sems):
    parts = [(tg, tg_via, tg_out)]
    for n in range(2):
        part = pl.ds(n * (HID // 2), HID // 2)
        parts.append((dg.at[part], dg_via.at[part], dg_out.at[part]))
    for n in range(4):
        part = pl.ds(n * (FEAT // 4), FEAT // 4)
        parts.append((gug.at[0, part], gug_via.at[0, part], gug_out.at[0, part]))
    here = [pltpu.make_async_copy(a, b, sems.at[0, n]) for n, (a, b, _) in enumerate(parts)]
    there = [pltpu.make_async_copy(b, c, sems.at[1, n]) for n, (_, b, c) in enumerate(parts)]
    for copy in here:
        copy.start()
    for first, then in zip(here, there):
        first.wait()
        then.start()
    for copy in there:
        copy.wait()


def local(tokens, d_out, row_expert, w_gate_up, w_down):
    vmem = pl.BlockSpec(memory_space=pltpu.VMEM)
    hbm = pl.BlockSpec(memory_space=pl.ANY)
    dma = pltpu.SemaphoreType.DMA

    def buf(count, width, kind=BF16):
        return pltpu.VMEM((count, width), kind)

    token_grads, gate_up_grads, down_grads = pl.pallas_call(
        kernel,
        out_shape=(
            jax.ShapeDtypeStruct((ROWS, FEAT), BF16),
            jax.ShapeDtypeStruct((1, FEAT, 2, HID), BF16),
            jax.ShapeDtypeStruct((HID, FEAT), BF16),
        ),
        in_specs=[vmem, vmem, vmem, hbm, hbm],
        out_specs=(vmem, hbm, hbm),
        scratch_shapes=[
            pltpu.VMEM((1, FEAT, 2, HID), BF16), buf(HID, FEAT),
            buf(FEAT, 2 * HID), buf(HID, FEAT),
            buf(SLOTS, FEAT), buf(SLOTS, FEAT),
            buf(BASE, FEAT), buf(BASE, FEAT),
            buf(2 * CAP, FEAT), buf(2 * CAP, FEAT),
            buf(BASE // 2, WIDE), buf(BASE // 2, WIDE),
            buf(BASE, WIDE, F32),
            buf(GROUPS * 6 * UNIT, WIDE), buf(GROUPS * 6 * UNIT, WIDE),
            buf(BASE, WIDE),
            buf(8 * QUARTER, 3 * TILE), buf(8 * QUARTER, 3 * TILE),
            buf(2 * BASE, 3 * TILE, F32),
            buf(8 * QUARTER, 3 * TILE), buf(6 * QUARTER, 3 * TILE),
            buf(2 * 6 * UNIT, 3 * TILE), buf(2 * 6 * UNIT, 3 * TILE),
            buf(2 * BASE, 3 * TILE),
            buf(SLOTS, FEAT), buf(BASE, FEAT), buf(BASE, FEAT),
            buf(CAP, FEAT), buf(CAP, FEAT),
            buf(8, ROWS, F32), buf(16, FEAT),
            dma((2,)), dma((2,)), dma((2, GROUPS)), dma((2, GROUPS)), dma((2,)), dma((2,)), dma((2,)), dma((2,)),
            dma((RINGS,)), dma((RINGS,)),
            dma((2, 3)), dma((2, 3)), dma((2, 3)), dma((2, 3)), dma((2, 3)), dma((2, 3)),
            dma((RINGS, 2, 4)), dma((RINGS, 2, 4)),
            dma((RINGS, 3, 4)), dma((RINGS, 2, 4)),
            dma, dma, dma, dma, dma, dma,
        ],
        compiler_params=pltpu.CompilerParams(
            collective_id=0, has_side_effects=True, vmem_limit_bytes=62 * 1024 * 1024
        ),
        cost_estimate=pl.CostEstimate(flops=15_000_000_000, bytes_accessed=14_000_000, transcendentals=131072),
        name="expert_backward",
    )(
        row_expert.reshape(1, ROWS), tokens, d_out,
        w_gate_up, w_down.reshape(HID, FEAT),
    )
    grads = (token_grads, gate_up_grads, down_grads.reshape(HID, FEAT))
    token_grads, gate_up_grads, down_grads = pl.pallas_call(
        hand_over,
        out_shape=tuple(jax.ShapeDtypeStruct(g.shape, g.dtype) for g in grads),
        in_specs=[hbm] * 3,
        out_specs=(hbm,) * 3,
        scratch_shapes=[buf(ROWS, FEAT), pltpu.VMEM((1, FEAT, 2, HID), BF16), buf(HID, FEAT), dma((2, 7))],
        name="hand_over",
    )(*grads)
    return token_grads, gate_up_grads, down_grads.reshape(1, HID, FEAT)


def solution(mesh):
    return jax.shard_map(
        local,
        mesh=mesh,
        in_specs=(
            P("exp", "grp"),
            P("exp", "grp"),
            P("exp"),
            P("exp", "grp", None, None),
            P("exp", None, "grp"),
        ),
        out_specs=(P("exp", "grp"), P("exp", "grp", None, None), P("exp", None, "grp")),
        check_vma=False,
    )
```

```python
import jax
import jax.numpy as jnp
from jax import lax
from jax.experimental import pallas as pl
from jax.experimental.pallas import tpu as pltpu
from jax.sharding import PartitionSpec as P

MESH = pl.DeviceIdType.MESH
F32 = jnp.float32
BF16 = jnp.bfloat16

ROWS = 256
FEAT = 896
HID = 1024
WIDE = 3 * HID
N_EXP = 32
HALF = 16
CAP = 16
BASE = N_EXP * CAP
SLOTS = 2 * BASE
GROUPS = 4
CHUNK = BASE // GROUPS
SHARE = CHUNK // 2
QUARTER = 64
UNIT = 16
TILE = 512
RINGS = 6

NN = (((1,), (0,)), ((), ()))
NT = (((1,), (1,)), ((), ()))
TN = (((0,), (0,)), ((), ()))


def mm(a, b, dims=NN):
    return lax.dot_general(a, b, dims, preferred_element_type=F32)


def rows(start, size):
    return pl.ds(pl.multiple_of(start, 16), size)


def kernel(
    expert_ref, tok_ref, dout_ref, wgu_hbm, wd_hbm,
    tg_ref, gug_hbm, dg_hbm,
    paired, down, wgu, wd, xin, din, sendx, sendd, ovx, ovd,
    csend, crecv, acc, rs_send, rs_recv, hb,
    ocsend, ocrecv, oacc, oxsend, oxrecv, ors_send, ors_recv, hbo,
    rowg, back, backo, zsend, zrecv, slots, hotm,
    w_sem, o_sem, base_send, base_recv, ovz_send, ovz_recv, ov_send, ov_recv,
    c_send, c_recv, x_send, x_recv, y_send, y_recv, yc_send, yc_recv,
    rs_s, rs_r, ag_s, ag_r, ret_s, ret_r, reto_s, reto_r, retz_s, retz_r,
):
    me_e = lax.axis_index("exp")
    me_g = lax.axis_index("grp")
    z = me_g // 2
    core = lax.rem(me_g, 2)
    half = me_e // HALF
    q = lax.rem(me_e, HALF)
    z_partner = {"exp": lax.rem(me_e + HALF, N_EXP)}
    core_partner = {"grp": me_g + 1 - 2 * core}
    x = lax.rem(me_e, 4)
    to_right = {"grp": lax.rem(me_g + 2, 8)}
    to_left = {"grp": lax.rem(me_g + 6, 8)}

    def remote(src, dst, s_sem, r_sem, dev):
        return pltpu.make_async_remote_copy(
            src_ref=src, dst_ref=dst, send_sem=s_sem, recv_sem=r_sem, device_id=dev, device_id_type=MESH
        )

    def peer(p, way):
        side = lax.rem(p // 4, 2)
        return lax.rem(half + side, 2) * HALF + lax.rem(q + HALF + way * ((p // 8) * 4 + lax.rem(p, 4)), HALF)

    w1 = pltpu.make_async_copy(wgu_hbm, paired, w_sem.at[0])
    w2 = pltpu.make_async_copy(wd_hbm, wd, w_sem.at[1])
    w1.start()
    w2.start()
    barrier = pltpu.get_barrier_semaphore()

    @pl.loop(1, N_EXP)
    def _(p):
        pl.semaphore_signal(
            barrier, inc=1, device_id={"exp": lax.rem(me_e + p, N_EXP)}, device_id_type=MESH
        )

    @pl.loop(1, 8)
    def _(p):
        pl.semaphore_signal(barrier, inc=1, device_id={"grp": lax.rem(me_g + p, 8)}, device_id_type=MESH)

    expert = expert_ref[...]
    e_iota = lax.broadcasted_iota(jnp.int32, (N_EXP, ROWS), 0)
    mine = (expert == e_iota).astype(F32)
    upto = (
        lax.broadcasted_iota(jnp.int32, (ROWS, ROWS), 0) <= lax.broadcasted_iota(jnp.int32, (ROWS, ROWS), 1)
    ).astype(F32).astype(BF16)
    running = mm(mine.astype(BF16), upto)
    rank = jnp.sum(running * mine, axis=0, keepdims=True) - 1.0
    slot = jnp.where(rank < CAP, expert.astype(F32) * CAP + rank, -1.0)
    over = rank - CAP
    slots[0:1, :] = slot
    slots[1:2, :] = over
    loads = jnp.sum(mine, axis=1, keepdims=True)
    is_me = (lax.broadcasted_iota(jnp.int32, (N_EXP, 1), 0) == me_e).astype(F32)
    hot = jnp.sum(jnp.where(loads > CAP + 0.5, 1.0, 0.0) * is_me, axis=0, keepdims=True)
    hotm[...] = jnp.broadcast_to(hot, (16, FEAT)).astype(BF16)

    def picks(start, size, values):
        at = lax.broadcasted_iota(jnp.int32, (size, ROWS), 0).astype(F32) + start
        return (at == values).astype(F32).astype(BF16)

    over_pick = picks(0.0, CAP, over)
    base_pick = picks(0.0, BASE, slot)
    for src, base, further in ((tok_ref, sendx, ovx), (dout_ref, sendd, ovd)):
        for c0, size in ((0, 256), (256, 256), (512, 256), (768, 128)):
            col = slice(c0, c0 + size)
            base[:, col] = mm(base_pick, src[:, col]).astype(BF16)
            further[0:CAP, col] = mm(over_pick, src[:, col]).astype(BF16)
    pl.semaphore_wait(barrier, N_EXP - 1 + 7)

    ovz = [
        remote(buf.at[pl.ds(0, CAP)], buf.at[pl.ds(CAP, CAP)], ovz_send.at[n], ovz_recv.at[n], z_partner)
        for n, buf in enumerate((ovx, ovd))
    ]
    for copy in ovz:
        copy.start()
    over_place = BASE + q * 2 * CAP

    def many(buf, count, s_sem, r_sem):
        part = buf.at[pl.ds(0, count)]
        return remote(part, part, s_sem, r_sem, z_partner)

    def base_block(k, p):
        to = peer(p, 1)
        for n, (src, dst) in enumerate(((sendx, xin), (sendd, din))):
            remote(
                src.at[rows(to * CAP, CAP)], dst.at[rows(p * CAP, CAP)],
                base_send.at[n, k], base_recv.at[n, k], {"exp": to},
            ).start()

    def further_block(first, p):
        to = half * HALF + lax.rem(q + p, HALF)
        for n, (src, dst) in enumerate(((ovx, xin), (ovd, din))):
            remote(
                src.at[pl.ds(first, CAP)], dst.at[rows(over_place + first, CAP)],
                ov_send.at[n], ov_recv.at[n], {"exp": to},
            ).start()

    def stage_d(k):
        @pl.loop(0, 8)
        def _(n):
            p = k * 8 + lax.rem(n + 4, 8)
            if k:
                base_block(k, p)
            else:

                @pl.when(p > 0)
                def _():
                    base_block(k, p)


    def left(k):
        for n, buf in enumerate((sendx, sendd)):
            many(buf, (8 if k else 7) * CAP, base_send.at[n, k], base_recv.at[n, k]).wait_send()

    @pl.loop(1, HALF)
    def _(p):
        further_block(0, p)

    stage_d(0)
    xin[0:CAP, :] = sendx[rows(me_e * CAP, CAP), :]
    din[0:CAP, :] = sendd[rows(me_e * CAP, CAP), :]
    w1.wait()

    @pl.loop(0, FEAT // 16)
    def _(n):
        at = rows(n * 16, 16)
        wgu[at, 0:HID] = paired[0, at, 0, :]
        wgu[at, HID:] = paired[0, at, 1, :]

    w2.wait()
    for copy in ovz:
        copy.wait_recv()

    @pl.loop(1, HALF)
    def _(p):
        further_block(CAP, p)

    stage_d(1)
    xin[rows(over_place, 2 * CAP), :] = ovx[...]
    din[rows(over_place, 2 * CAP), :] = ovd[...]

    def base_rows(k):
        for n, buf in enumerate((xin, din)):
            many(buf, (8 if k else 7) * CAP, base_send.at[n, k], base_recv.at[n, k]).wait_recv()

    def core_copy(n):
        src, dst = (csend, crecv) if n < GROUPS else (ocsend, ocrecv)
        part = pl.ds(n * SHARE, SHARE) if n < GROUPS else pl.ds((n - GROUPS) * 4 * QUARTER, 4 * QUARTER)
        return remote(src.at[part], dst.at[part], c_send.at[n], c_recv.at[n], core_partner)

    def stage_p(k):
        here = pl.ds(k * CHUNK, CHUNK)

        @pl.loop(0, 2 * HID // TILE)
        def _(n):
            col = pl.ds(pl.multiple_of(n * TILE, TILE), TILE)
            acc[here, col] = mm(xin[here, :], wgu[:, col])

        @pl.loop(0, HID // TILE)
        def _(n):
            col = pl.ds(pl.multiple_of(2 * HID + n * TILE, TILE), TILE)
            acc[here, col] = mm(din[here, :], wd[rows(n * TILE, TILE), :], NT)

        @pl.loop(0, SHARE // 16)
        def _(n):
            theirs = rows(k * CHUNK + (1 - core) * SHARE + n * 16, 16)
            csend[rows(k * SHARE + n * 16, 16), :] = acc[theirs, :].astype(BF16)

        core_copy(k).start()

    def stage_c(k):
        core_copy(k).wait_recv()

        @pl.loop(0, SHARE // 16)
        def _(n):
            mine = rows(k * CHUNK + core * SHARE + n * 16, 16)
            acc[mine, :] += crecv[rows(k * SHARE + n * 16, 16), :].astype(F32)

    def stage_po(h):
        @pl.loop(0, BASE // 128)
        def _(n):
            rows_in = xin[rows(BASE + n * 128, 128), :]
            grads_in = din[rows(BASE + n * 128, 128), :]
            here = rows(h * BASE + n * 128, 128)
            oacc[here, 0:TILE] = mm(rows_in, wgu[:, h * TILE : (h + 1) * TILE])
            oacc[here, TILE : 2 * TILE] = mm(rows_in, wgu[:, HID + h * TILE : HID + (h + 1) * TILE])
            oacc[here, 2 * TILE :] = mm(grads_in, wd[h * TILE : (h + 1) * TILE, :], NT)

        @pl.loop(0, 4 * QUARTER // 16)
        def _(n):
            theirs = rows(h * BASE + (1 - core) * 4 * QUARTER + n * 16, 16)
            ocsend[rows(h * 4 * QUARTER + n * 16, 16), :] = oacc[theirs, :].astype(BF16)

        core_copy(GROUPS + h).start()

    y = q // 4
    spot = (x, y)

    def along(h, p):
        return {"exp": me_e - x + lax.rem(x + p, 4) if h == 0 else me_e - 4 * y + 4 * lax.rem(y + p, 4)}

    def x_copy(h, p):
        return remote(
            oxsend.at[rows(h * 4 * QUARTER + lax.rem(spot[h] + p, 4) * QUARTER, QUARTER)],
            oxrecv.at[pl.ds((h * 3 + p - 1) * QUARTER, QUARTER)],
            x_send.at[h, p - 1], x_recv.at[h, p - 1], along(h, p),
        )

    def stage_co(h):
        core_copy(GROUPS + h).wait_recv()

        @pl.loop(0, 4 * QUARTER // 16)
        def _(n):
            mine = rows(h * BASE + core * 4 * QUARTER + n * 16, 16)
            here = rows(h * 4 * QUARTER + n * 16, 16)
            value = oacc[mine, :] + ocrecv[here, :].astype(F32)
            oacc[mine, :] = value
            oxsend[here, :] = value.astype(BF16)

        for p in (1, 2, 3):
            x_copy(h, p).start()

    def stage_xo(h):
        for p in (1, 2, 3):
            x_copy(h, p).wait_recv()

        @pl.loop(0, QUARTER // 16)
        def _(n):
            at = rows(h * BASE + further_row(spot[h], core) + n * 16, 16)
            value = oacc[at, :]
            for p in range(3):
                value = value + oxrecv[rows((h * 3 + p) * QUARTER + n * 16, 16), :].astype(F32)
            oacc[at, :] = value

    def ring(r):
        if r < GROUPS:
            return acc, rs_send, rs_recv, hb, r * 6, HID
        return oacc, ors_send, ors_recv, hbo, (r - GROUPS) * 6, TILE

    def block_row(r, c, j):
        if r < GROUPS:
            return r * CHUNK + c * SHARE + j * UNIT
        return (r - GROUPS) * BASE + further_row(spot[r - GROUPS], c) + j * UNIT

    def further_row(at, c):
        return c * 4 * QUARTER + at * QUARTER

    def rs_copy(r, way, d):
        _, send, recv, _, first, _ = ring(r)
        part = rows((first + way * 3 + d - 1 + way) * UNIT, UNIT)
        return remote(send.at[part], recv.at[part], rs_s.at[r, way, d], rs_r.at[r, way, d], (to_right, to_left)[way])

    def rs_forward(r, way, d, start):
        total, send, recv, _, first, _ = ring(r)
        part = pl.ds((first + way * 3 + d - 1 + way) * UNIT, UNIT)
        copy = rs_copy(r, way, d)
        value = total[rows(block_row(r, core, d), UNIT), :]
        if not start:
            copy.wait_recv()
            value = value + recv[part, :].astype(F32)
        send[part, :] = value.astype(BF16)
        copy.start()

    def stage_e(r):
        @pl.when(z == 0)
        def _():
            for d in (3, 2, 1):
                rs_forward(r, 0, d, True)

        @pl.when(z == 3)
        def _():
            for d in (0, 1, 2):
                rs_forward(r, 1, d, True)

    def stage_m1(r):
        @pl.when(z == 1)
        def _():
            rs_forward(r, 0, 3, False)

        @pl.when(z == 2)
        def _():
            rs_forward(r, 1, 0, False)

    def stage_m2(r):
        @pl.when(z == 1)
        def _():
            rs_forward(r, 0, 2, False)
            rs_forward(r, 1, 0, False)

        @pl.when(z == 2)
        def _():
            rs_forward(r, 1, 1, False)
            rs_forward(r, 0, 3, False)

    def ag_copy(r, way, j):
        out = ring(r)[3]
        part = rows(block_row(r, core, j), UNIT)
        return remote(
            out.at[part], out.at[part], ag_s.at[r, way, j], ag_r.at[r, core, j], (to_right, to_left, core_partner)[way]
        )

    def stage_f(r):
        total, _, recv, out, first, wide = ring(r)
        at = rows(block_row(r, core, z), UNIT)

        def fold(way):
            rs_copy(r, way, z).wait_recv()
            total[at, :] += recv[rows((first + way * 3 + z - 1 + way) * UNIT, UNIT), :].astype(F32)

        @pl.when(z > 0)
        def _():
            fold(0)

        @pl.when(z < 3)
        def _():
            fold(1)

        @pl.loop(0, wide // 256)
        def _(n):
            c0 = pl.multiple_of(n * 256, 256)
            gate = total[at, pl.ds(c0, 256)]
            up = total[at, pl.ds(c0 + wide, 256)]
            grad = total[at, pl.ds(c0 + 2 * wide, 256)]
            sig = jax.nn.sigmoid(gate)
            act = gate * sig
            slope = sig * (1.0 + gate * (1.0 - sig))
            out[at, pl.ds(c0, 256)] = (act * up).astype(BF16)
            out[at, pl.ds(c0 + wide, 256)] = (grad * up * slope).astype(BF16)
            out[at, pl.ds(c0 + 2 * wide, 256)] = (grad * act).astype(BF16)

        @pl.when(z < 3)
        def _():
            ag_copy(r, 0, z).start()

        @pl.when(z > 0)
        def _():
            ag_copy(r, 1, z).start()

        ag_copy(r, 2, z).start()

    def stage_a(r, dist):
        from_left = z - dist
        from_right = z + dist

        @pl.when(from_left >= 0)
        def _():
            ag_copy(r, 0, from_left).wait_recv()

            @pl.when(z < 3)
            def _():
                ag_copy(r, 0, from_left).start()

            ag_copy(r, 2, from_left).start()

        @pl.when(from_right <= 3)
        def _():
            ag_copy(r, 1, from_right).wait_recv()

            @pl.when(z > 0)
            def _():
                ag_copy(r, 1, from_right).start()

            ag_copy(r, 2, from_right).start()

    def y_copy(h, p):
        part = rows(h * BASE + further_row(spot[h], core), QUARTER)
        return remote(hbo.at[part], hbo.at[part], y_send.at[h, p - 1], y_recv.at[h, p - 1], along(h, p))

    def yc_copy(h, p, c):
        part = rows(h * BASE + further_row(lax.rem(spot[h] + 4 - p, 4), c), QUARTER)
        return remote(hbo.at[part], hbo.at[part], yc_send.at[h, p - 1], yc_recv.at[h, p - 1], core_partner)

    def stage_z(h):
        for p in (1, 2, 3):
            y_copy(h, p).start()

    def stage_y(h):
        for p in (1, 2, 3):
            y_copy(h, p).wait_recv()
            yc_copy(h, p, core).start()

    def from_core(r):
        out = ring(r)[3]
        for j in range(4):
            part = rows(block_row(r, 1 - core, j), UNIT)
            remote(
                out.at[part], out.at[part], ag_s.at[r, 2, j], ag_r.at[r, 1 - core, j], core_partner
            ).wait_recv()

    def stage_g(k):
        from_core(k)
        here = pl.ds(k * CHUNK, CHUNK)
        for c0, size in ((0, 256), (256, 256), (512, 256), (768, 128)):
            rowg[here, c0 : c0 + size] = mm(hb[here, HID:], wgu[c0 : c0 + size, :], NT).astype(BF16)

        @pl.loop(k * 8 if k else 1, k * 8 + 8)
        def _(p):
            to = peer(p, -1)
            remote(
                rowg.at[rows(p * CAP, CAP)], back.at[rows(me_e * CAP, CAP)], ret_s, ret_r, {"exp": to}
            ).start()

        if k == 0:
            back[rows(me_e * CAP, CAP), :] = rowg[0:CAP, :]

    def stage_go():
        for h in range(2):
            from_core(GROUPS + h)
            for p in (1, 2, 3):
                yc_copy(h, p, 1 - core).wait_recv()

        @pl.loop(0, 2)
        def _(n):
            for c0, size in ((0, 256), (256, 256), (512, 256), (768, 128)):
                value = jnp.zeros((256, size), F32)
                for h in range(2):
                    for b in range(2):
                        value = value + mm(
                            hbo[rows(h * BASE + n * 256, 256), (1 + b) * TILE : (2 + b) * TILE],
                            wgu[c0 : c0 + size, b * HID + h * TILE : b * HID + (h + 1) * TILE], NT,
                        )
                value = value * hotm[0:1, c0 : c0 + size].astype(F32)
                rowg[rows(BASE + n * 256, 256), c0 : c0 + size] = value.astype(BF16)

            @pl.loop(0, 8)
            def _(p):
                near = n * 8 + lax.rem(q + p, 8)

                @pl.when(near != q)
                def _():
                    remote(
                        rowg.at[rows(BASE + near * 2 * CAP, 2 * CAP)], backo.at[rows(q * 2 * CAP, 2 * CAP)],
                        reto_s, reto_r, {"exp": half * HALF + near},
                    ).start()

        backo[rows(q * 2 * CAP, 2 * CAP), :] = rowg[rows(BASE + q * 2 * CAP, 2 * CAP), :]

    def hot_rows():
        many(xin, (HALF - 1) * 2 * CAP, ov_send.at[0], ov_recv.at[0]).wait_recv()
        many(din, (HALF - 1) * 2 * CAP, ov_send.at[1], ov_recv.at[1]).wait_recv()

        @pl.loop(0, BASE // 16)
        def _(n):
            at = rows(BASE + n * 16, 16)
            xin[at, :] = xin[at, :] * hotm[...]
            din[at, :] = din[at, :] * hotm[...]

    left(0)
    stage_d(2)
    base_rows(0)
    stage_p(0)
    stage_c(0)
    stage_e(0)
    left(1)
    stage_d(3)
    base_rows(1)
    stage_p(1)
    stage_c(1)
    stage_e(1)
    hot_rows()
    stage_po(0)
    stage_m1(0)
    stage_po(1)
    stage_m1(1)
    stage_co(0)
    stage_co(1)
    stage_m2(0)
    stage_m2(1)
    stage_f(0)
    stage_f(1)
    base_rows(2)
    stage_p(2)
    stage_c(2)
    stage_xo(0)
    stage_xo(1)
    stage_e(4)
    stage_e(5)
    stage_a(0, 1)
    stage_a(1, 1)
    stage_m1(4)
    stage_m1(5)
    stage_a(0, 2)
    stage_a(1, 2)
    stage_m2(4)
    stage_m2(5)
    stage_e(2)
    stage_a(0, 3)
    stage_a(1, 3)
    stage_f(4)
    stage_f(5)
    base_rows(3)
    stage_p(3)
    stage_c(3)
    stage_e(3)
    stage_m1(2)
    stage_a(4, 1)
    stage_a(5, 1)
    stage_m1(3)
    stage_a(4, 2)
    stage_a(5, 2)
    stage_m2(2)
    stage_m2(3)
    stage_a(4, 3)
    stage_z(0)
    stage_a(5, 3)
    stage_z(1)
    stage_f(2)
    stage_f(3)
    stage_g(0)
    stage_a(2, 1)
    stage_a(3, 1)
    stage_y(0)
    stage_y(1)
    stage_go()
    stage_a(2, 2)
    stage_a(3, 2)
    stage_a(2, 3)
    stage_g(2)
    stage_g(1)
    stage_a(3, 3)
    stage_g(3)

    def gate_up_grads():
        for b in range(2):

            @pl.loop(0, HID // TILE)
            def _(n):
                c0 = pl.multiple_of(n * TILE, TILE)
                near = hb[:, pl.ds(c0 + HID * (1 + b), TILE)]
                further = hbo[rows(n * BASE, BASE), (1 + b) * TILE : (2 + b) * TILE]
                for f0, size in ((0, 256), (256, 256), (512, 256), (768, 128)):
                    value = mm(xin[0:BASE, f0 : f0 + size], near, TN)
                    value = value + mm(xin[BASE:, f0 : f0 + size], further, TN)
                    paired[0, f0 : f0 + size, b, pl.ds(c0, TILE)] = value.astype(BF16)

    def down_grads():
        for h in range(2):

            @pl.loop(0, 2)
            def _(n):
                c0 = pl.multiple_of(n * 256, 256)
                value = mm(hb[:, pl.ds(c0 + h * TILE, 256)], din[0:BASE, :], TN)
                value = value + mm(hbo[h * BASE : (h + 1) * BASE, pl.ds(c0, 256)], din[BASE:, :], TN)
                down[pl.ds(c0 + h * TILE, 256), :] = value.astype(BF16)

    out_down = pltpu.make_async_copy(down, dg_hbm, o_sem.at[0])
    out_gate_up = pltpu.make_async_copy(paired, gug_hbm, o_sem.at[1])
    gate_up_grads()
    out_gate_up.start()
    many(backo, (HALF - 1) * 2 * CAP, reto_s, reto_r).wait_recv()
    for c0 in (0, CAP):
        total = jnp.zeros((CAP, FEAT), F32)
        for n in range(HALF):
            total = total + backo[n * 2 * CAP + c0 : n * 2 * CAP + c0 + CAP, :].astype(F32)
        if c0:
            zsend[...] = total.astype(BF16)
        else:
            ovx_total = total
    back_z = remote(zsend, zrecv, retz_s, retz_r, z_partner)
    back_z.start()
    down_grads()
    out_down.start()
    many(back, BASE - CAP, ret_s, ret_r).wait_recv()
    back_z.wait_recv()
    over_rows = (ovx_total + zrecv[...].astype(F32)).astype(BF16)
    over_at = picks(0.0, CAP, slots[1:2, :])
    total = mm(over_at, over_rows, TN)
    for b in range(BASE // 128):
        pick = picks(128.0 * b, 128, slots[0:1, :])
        total = total + mm(pick, back[b * 128 : (b + 1) * 128, :], TN)
    tg_ref[...] = total.astype(BF16)

    out_down.wait()
    out_gate_up.wait()
    for copy in ovz:
        copy.wait_send()
    left(2)
    left(3)
    for n in range(2):
        many(xin, (HALF - 1) * 2 * CAP, ov_send.at[n], ov_recv.at[n]).wait_send()
    many(rowg, BASE - CAP, ret_s, ret_r).wait_send()
    many(rowg, (HALF - 1) * 2 * CAP, reto_s, reto_r).wait_send()
    back_z.wait_send()
    for n in range(RINGS):
        core_copy(n).wait_send()
    for h in range(2):
        for p in (1, 2, 3):
            x_copy(h, p).wait_send()
            y_copy(h, p).wait_send()
            yc_copy(h, p, core).wait_send()
    for r in range(RINGS):
        for d in range(4):
            if d > 0:

                @pl.when(z < d)
                def _():
                    rs_copy(r, 0, d).wait_send()

            if d < 3:

                @pl.when(z > d)
                def _():
                    rs_copy(r, 1, d).wait_send()

            @pl.when(jnp.logical_and(z >= d, z < 3))
            def _():
                ag_copy(r, 0, d).wait_send()

            @pl.when(jnp.logical_and(z <= d, z > 0))
            def _():
                ag_copy(r, 1, d).wait_send()

            ag_copy(r, 2, d).wait_send()


def hand_over(tg, gug, dg, tg_out, gug_out, dg_out, tg_via, gug_via, dg_via, sems):
    parts = [(tg, tg_via, tg_out)]
    for n in range(2):
        part = pl.ds(n * (HID // 2), HID // 2)
        parts.append((dg.at[part], dg_via.at[part], dg_out.at[part]))
    for n in range(4):
        part = pl.ds(n * (FEAT // 4), FEAT // 4)
        parts.append((gug.at[0, part], gug_via.at[0, part], gug_out.at[0, part]))
    here = [pltpu.make_async_copy(a, b, sems.at[0, n]) for n, (a, b, _) in enumerate(parts)]
    there = [pltpu.make_async_copy(b, c, sems.at[1, n]) for n, (_, b, c) in enumerate(parts)]
    for copy in here:
        copy.start()
    for first, then in zip(here, there):
        first.wait()
        then.start()
    for copy in there:
        copy.wait()


def local(tokens, d_out, row_expert, w_gate_up, w_down):
    vmem = pl.BlockSpec(memory_space=pltpu.VMEM)
    hbm = pl.BlockSpec(memory_space=pl.ANY)
    dma = pltpu.SemaphoreType.DMA

    def buf(count, width, kind=BF16):
        return pltpu.VMEM((count, width), kind)

    token_grads, gate_up_grads, down_grads = pl.pallas_call(
        kernel,
        out_shape=(
            jax.ShapeDtypeStruct((ROWS, FEAT), BF16),
            jax.ShapeDtypeStruct((1, FEAT, 2, HID), BF16),
            jax.ShapeDtypeStruct((HID, FEAT), BF16),
        ),
        in_specs=[vmem, vmem, vmem, hbm, hbm],
        out_specs=(vmem, hbm, hbm),
        scratch_shapes=[
            pltpu.VMEM((1, FEAT, 2, HID), BF16), buf(HID, FEAT),
            buf(FEAT, 2 * HID), buf(HID, FEAT),
            buf(SLOTS, FEAT), buf(SLOTS, FEAT),
            buf(BASE, FEAT), buf(BASE, FEAT),
            buf(2 * CAP, FEAT), buf(2 * CAP, FEAT),
            buf(BASE // 2, WIDE), buf(BASE // 2, WIDE),
            buf(BASE, WIDE, F32),
            buf(GROUPS * 6 * UNIT, WIDE), buf(GROUPS * 6 * UNIT, WIDE),
            buf(BASE, WIDE),
            buf(8 * QUARTER, 3 * TILE), buf(8 * QUARTER, 3 * TILE),
            buf(2 * BASE, 3 * TILE, F32),
            buf(8 * QUARTER, 3 * TILE), buf(6 * QUARTER, 3 * TILE),
            buf(2 * 6 * UNIT, 3 * TILE), buf(2 * 6 * UNIT, 3 * TILE),
            buf(2 * BASE, 3 * TILE),
            buf(SLOTS, FEAT), buf(BASE, FEAT), buf(BASE, FEAT),
            buf(CAP, FEAT), buf(CAP, FEAT),
            buf(8, ROWS, F32), buf(16, FEAT),
            dma((2,)), dma((2,)), dma((2, GROUPS)), dma((2, GROUPS)), dma((2,)), dma((2,)), dma((2,)), dma((2,)),
            dma((RINGS,)), dma((RINGS,)),
            dma((2, 3)), dma((2, 3)), dma((2, 3)), dma((2, 3)), dma((2, 3)), dma((2, 3)),
            dma((RINGS, 2, 4)), dma((RINGS, 2, 4)),
            dma((RINGS, 3, 4)), dma((RINGS, 2, 4)),
            dma, dma, dma, dma, dma, dma,
        ],
        compiler_params=pltpu.CompilerParams(
            collective_id=0, has_side_effects=True, vmem_limit_bytes=62 * 1024 * 1024
        ),
        cost_estimate=pl.CostEstimate(flops=15_000_000_000, bytes_accessed=14_000_000, transcendentals=131072),
        name="expert_backward",
    )(
        row_expert.reshape(1, ROWS), tokens, d_out,
        w_gate_up, w_down.reshape(HID, FEAT),
    )
    grads = (token_grads, gate_up_grads, down_grads.reshape(HID, FEAT))
    token_grads, gate_up_grads, down_grads = pl.pallas_call(
        hand_over,
        out_shape=tuple(jax.ShapeDtypeStruct(g.shape, g.dtype) for g in grads),
        in_specs=[hbm] * 3,
        out_specs=(hbm,) * 3,
        scratch_shapes=[buf(ROWS, FEAT), pltpu.VMEM((1, FEAT, 2, HID), BF16), buf(HID, FEAT), dma((2, 7))],
        name="hand_over",
    )(*grads)
    return token_grads, gate_up_grads, down_grads.reshape(1, HID, FEAT)


def solution(mesh):
    return jax.shard_map(
        local,
        mesh=mesh,
        in_specs=(
            P("exp", "grp"),
            P("exp", "grp"),
            P("exp"),
            P("exp", "grp", None, None),
            P("exp", None, "grp"),
        ),
        out_specs=(P("exp", "grp"), P("exp", "grp", None, None), P("exp", None, "grp")),
        check_vma=False,
    )
```
